32 devices in a mesh: groups: 2 (over x), wide: 4 (over y, core), narrow: 4 (over z).
Axes of the slice: x: 2, y: 2, z: 4, core: 2. Of those that a mesh axis runs over, the one named last changes fastest.
Arguments:
- density: bfloat16 [3072, 1536], P(('groups', 'wide'), 'narrow'), parts along dimension 0, as said below
- pattern: int32 [96, 48], P(('groups', 'wide'), 'narrow'), parts along dimension 0, may hold values from 0 to 1, as said below
Outputs:
- purified: bfloat16 [3072, 1536], P(('groups', 'wide'), 'narrow'), parts along dimension 0
The draws below stay inside these ranges and needn't reach their ends.
There are 2 independent parts, one for each index of `groups`. The reference program is written for one: setup_inputs(seed, part) draws one part's arguments, and reference() takes and returns one part's arrays. A program takes and returns all parts, laid end to end along the dimension named above; each array names one. Nothing has to cross between parts.
Inputs may be any that keep to these rules, and one draw needn't show every extreme that they name: density is symmetric and zero outside the blocks that pattern marks. pattern is symmetric; the blocks on the diagonal are always occupied.
All inputs are finite; a program needn't handle non-finite values.
Results may differ from the reference program's by a relative error of at most 0.0055.
Values may be sent and summed in bfloat16 or wider, within the bound.
No kernel may reach another device: no remote copies, remote signals or barrier semaphores. Data moves between devices by JAX's collectives and lax.ppermute only.
A program may use at most 64 MiB of HBM per device.

```python
import jax
import jax.numpy as jnp
from jax import lax

BLOCK = 32
NB = 48
ORDER = 1536


def occupancy(key):
    raw_draw = jax.random.randint(key, (NB, NB), 0, 1000)
    row_index = lax.broadcasted_iota(jnp.int32, (NB, NB), 0)
    col_index = lax.broadcasted_iota(jnp.int32, (NB, NB), 1)
    upper = jnp.where(row_index <= col_index, raw_draw, raw_draw.T)
    occupied = (upper < 450) | (row_index == col_index)
    return jnp.where(occupied, 1, 0).astype(jnp.int32)


def draw_pattern(key, part):
    return occupancy(key)


def draw_density(key, part):
    occupied = occupancy(key)
    key = jax.random.fold_in(key, 3)
    first_key = jax.random.fold_in(key, 0)
    spread_scale = 1.2 * (0.45 * ORDER) ** (-0.5)
    values = jax.random.normal(first_key, (ORDER, ORDER), jnp.float32)
    row_index = lax.broadcasted_iota(jnp.int32, (ORDER, ORDER), 0)
    col_index = lax.broadcasted_iota(jnp.int32, (ORDER, ORDER), 1)
    values = jnp.where(row_index <= col_index, values, values.T) * spread_scale
    values = values + jnp.where(row_index == col_index, 0.5, 0.0).astype(jnp.float32)
    tile_mask = jnp.repeat(jnp.repeat(occupied, BLOCK, 0), BLOCK, 1).astype(jnp.float32)
    return (values * tile_mask).astype(jnp.bfloat16)


def setup_inputs(seed: int = 0, part: int = 0) -> dict:
    streams_of = jax.random.split(jax.random.key(seed), 3)
    part_keys = jax.random.split(jax.random.fold_in(streams_of[2], part), 3)
    return {
        "density": draw_density(jax.random.fold_in(jax.random.fold_in(streams_of[2], part), 71), part),
        "pattern": draw_pattern(jax.random.fold_in(jax.random.fold_in(streams_of[2], part), 71), part),
    }


def reference(density, pattern):
    tile_mask = jnp.repeat(jnp.repeat(pattern, BLOCK, 0), BLOCK, 1).astype(jnp.float32)
    square = jnp.dot(density, density, preferred_element_type=jnp.float32) * tile_mask
    square_low = square.astype(jnp.bfloat16)
    cube_sum = jnp.dot(square_low, density, preferred_element_type=jnp.float32) * tile_mask
    return (3.0 * square - 2.0 * cube_sum).astype(jnp.bfloat16)
```

```python
import functools

import jax
import jax.numpy as jnp
import numpy as np
from jax import lax
from jax.experimental import pallas as pl
from jax.experimental.pallas import tpu as pltpu
from jax.sharding import PartitionSpec as P

AXES = ("wide", "narrow")
F32, BF16 = jnp.float32, jnp.bfloat16


def expand(pattern, row_count, col_count):
    block_rows, block_cols = pattern.shape
    block_edge = row_count // block_rows
    spread_out = jnp.broadcast_to(
        pattern[:, None, :, None], (block_rows, block_edge, block_cols, block_edge)
    )
    return spread_out.reshape(row_count, col_count).astype(jnp.float32)


def panel_body(density, pattern):
    row_count, col_count = density.shape
    tile_mask = expand(pattern, row_count, col_count)
    row_panel = lax.all_gather(density, "narrow", axis=1, tiled=True)
    col_panel = lax.all_gather(density, "wide", axis=0, tiled=True)
    square = jnp.dot(row_panel, col_panel, preferred_element_type=F32) * tile_mask
    square_low = square.astype(BF16)
    square_panel = lax.all_gather(square_low, "narrow", axis=1, tiled=True)
    cube_sum = jnp.dot(square_panel, col_panel, preferred_element_type=F32) * tile_mask
    return (3.0 * square - 2.0 * cube_sum).astype(BF16)


def number(i, j):
    return 4 * i + j


def turned(moves):
    other = [((3 - a, 3 - b), (3 - c, 3 - d)) for (a, b), (c, d) in moves]
    return [(number(*s), number(*t)) for s, t in moves + other]


def swap_rows(bit):
    return [(number(i, j), number(i ^ bit, j)) for i in range(4) for j in range(4)]


LINE = turned(
    [
        ((2, 0), (2, 3)),
        ((2, 1), (3, 3)),
        ((3, 0), (2, 2)),
        ((3, 1), (3, 2)),
        ((2, 2), (2, 1)),
        ((3, 2), (3, 1)),
        ((2, 3), (2, 0)),
        ((3, 3), (3, 0)),
    ]
)
ACROSS = swap_rows(2)
CORES = swap_rows(1)
PAIRS = [(number(i, j), number(i, j ^ 1)) for i in range(4) for j in range(4)]


def send(array, moves):
    return lax.ppermute(array, AXES, moves)


def moved(names, moves):
    out = [None] * 16
    for source, target in moves:
        out[target] = names[source]
    return out


def whose_blocks():
    own = [(i, j) for i in range(4) for j in range(4)]
    line = moved(own, LINE)
    across = moved(own, ACROSS)
    line_across = moved(line, ACROSS)
    by_class = [own, line_across, across, line]
    picked = [by_class[(d // 4) ^ (d % 4)][d] for d in range(16)]
    pairs = moved(picked, PAIRS)
    mine = [own, across, line, line_across, pairs]
    theirs = [moved(names, CORES) for names in mine]
    table = np.array([[x[d] for x in mine + theirs] for d in range(16)], np.int32)
    for d in range(16):
        assert len({tuple(sorted(ab)) for ab in table[d].tolist()}) == 10
    return table.reshape(16, 20)


def pack_kernel(density, pattern, out):
    rows = density.shape[0]
    n = pattern.shape[0]
    out[:rows] = density[...]
    tile = out.shape[0] - rows
    r = lax.broadcasted_iota(jnp.int32, (tile, n), 0)
    c = lax.broadcasted_iota(jnp.int32, (tile, n), 1)
    left = jnp.where(r == c, 1.0, 0.0).astype(F32)
    r = lax.broadcasted_iota(jnp.int32, (n, 128), 0)
    c = lax.broadcasted_iota(jnp.int32, (n, 128), 1)
    right = jnp.where(r == c, 1.0, 0.0).astype(F32)
    p = pattern[...].astype(F32)
    plain = jnp.dot(jnp.dot(left, p), right)
    flipped = jnp.dot(
        lax.dot_general(left, p, (((1,), (1,)), ((), ())), preferred_element_type=F32), right
    )
    out[rows:] = jnp.zeros_like(out[rows:])
    out[rows:, 0:128] = plain.astype(BF16)
    out[rows:, 128:256] = flipped.astype(BF16)


def purify_kernel(n, where, *refs):
    blocks, out, full, mask, square, low = refs[:10], refs[10], *refs[11:]
    edge = out.shape[0]
    order = full.shape[0]
    step = edge // n
    i, j = where[20], where[21]
    r = lax.broadcasted_iota(jnp.int32, (128, edge), 0)
    c = lax.broadcasted_iota(jnp.int32, (128, edge), 1)
    widen = jnp.where(r == c // step, 1.0, 0.0).astype(BF16)

    def at(k):
        return pl.ds(pl.multiple_of(k * edge, 128), edge)

    def put_mask(small, k):
        rows = jnp.dot(small, widen, preferred_element_type=F32)[:n]
        tall = jnp.broadcast_to(rows[:, None, :], (n, step, edge)).reshape(edge, edge)
        mask[:, at(k)] = tall

    for k, ref in enumerate(blocks):
        a, b = where[2 * k], where[2 * k + 1]
        block = ref[:edge]
        full[at(a), at(b)] = block

        @pl.when(a != b)
        def _():
            full[at(b), at(a)] = block.T

        @pl.when(a == i)
        def _():
            put_mask(ref[edge:, 0:128], b)

        @pl.when((b == i) & (a != b))
        def _():
            put_mask(ref[edge:, 128:256], a)

    panel = full[at(i)]
    width = 256
    for t in range(order // width):
        cols = slice(t * width, (t + 1) * width)
        s = jnp.dot(panel, full[:, cols], preferred_element_type=F32) * mask[:, cols]
        square[:, cols] = s
        low[:, cols] = s.astype(BF16)
    cube = jnp.dot(low[...], full[:, at(j)], preferred_element_type=F32) * mask[:, at(j)]
    out[...] = (3.0 * square[:, at(j)] - 2.0 * cube).astype(BF16)


def block_body(density, pattern):
    edge = density.shape[0]
    order = 4 * edge
    n = pattern.shape[0]
    vmem = pl.BlockSpec(memory_space=pltpu.VMEM)
    own = pl.pallas_call(
        pack_kernel,
        out_shape=jax.ShapeDtypeStruct((edge + 16, edge), BF16),
        in_specs=[vmem] * 2,
        out_specs=vmem,
        name="pack",
    )(density, pattern)
    i, j = lax.axis_index("wide"), lax.axis_index("narrow")
    hold = lax.optimization_barrier
    line, across, own_c = send(own, LINE), send(own, ACROSS), send(own, CORES)
    line, across, own_c = hold((line, across, own_c))
    line_across = send(line, ACROSS)
    line_c, across_c = send(line, CORES), send(across, CORES)
    line_across, line_c, across_c = hold((line_across, line_c, across_c))
    kind = jnp.bitwise_xor(i, j)
    picked = jnp.where(
        kind == 0, own, jnp.where(kind == 1, line_across, jnp.where(kind == 2, across, line))
    )
    pairs = send(picked, PAIRS)
    line_across_c = send(line_across, CORES)
    pairs_c = send(pairs, CORES)
    table = jnp.asarray(whose_blocks())
    where = jnp.concatenate([table[number(i, j)], jnp.stack([i, j]).astype(jnp.int32)])
    return pl.pallas_call(
        functools.partial(purify_kernel, n),
        out_shape=jax.ShapeDtypeStruct((edge, edge), BF16),
        in_specs=[pl.BlockSpec(memory_space=pltpu.SMEM)] + [vmem] * 10,
        out_specs=vmem,
        scratch_shapes=[
            pltpu.VMEM((order, order), BF16),
            pltpu.VMEM((edge, order), F32),
            pltpu.VMEM((edge, order), F32),
            pltpu.VMEM((edge, order), BF16),
        ],
        compiler_params=pltpu.CompilerParams(vmem_limit_bytes=40 << 20),
        name="purify",
    )(where, own, across, line, line_across, pairs, own_c, across_c, line_c, line_across_c, pairs_c)


def solution(mesh):
    four = mesh.shape["wide"] == 4 and mesh.shape["narrow"] == 4

    def body(density, pattern):
        rows, cols = density.shape
        fits = rows == cols and rows % 128 == 0 and rows <= 512
        fits = fits and pattern.shape[0] == pattern.shape[1] <= 16
        return (block_body if four and fits else panel_body)(density, pattern)

    return jax.shard_map(
        body,
        mesh=mesh,
        in_specs=(P(("groups", "wide"), "narrow"), P(("groups", "wide"), "narrow")),
        out_specs=P(("groups", "wide"), "narrow"),
        check_vma=False,
    )
```

```python
import jax
import jax.numpy as jnp
import numpy as np
from jax import lax
from jax.experimental import pallas as pl
from jax.experimental.pallas import tpu as pltpu
from jax.sharding import PartitionSpec as P

AXES = ("wide", "narrow")
F32, BF16 = jnp.float32, jnp.bfloat16


def expand(pattern, row_count, col_count):
    block_rows, block_cols = pattern.shape
    block_edge = row_count // block_rows
    spread_out = jnp.broadcast_to(
        pattern[:, None, :, None], (block_rows, block_edge, block_cols, block_edge)
    )
    return spread_out.reshape(row_count, col_count).astype(jnp.float32)


def panel_body(density, pattern):
    row_count, col_count = density.shape
    tile_mask = expand(pattern, row_count, col_count)
    row_panel = lax.all_gather(density, "narrow", axis=1, tiled=True)
    col_panel = lax.all_gather(density, "wide", axis=0, tiled=True)
    square = jnp.dot(row_panel, col_panel, preferred_element_type=F32) * tile_mask
    square_low = square.astype(BF16)
    square_panel = lax.all_gather(square_low, "narrow", axis=1, tiled=True)
    cube_sum = jnp.dot(square_panel, col_panel, preferred_element_type=F32) * tile_mask
    return (3.0 * square - 2.0 * cube_sum).astype(BF16)


def number(i, j):
    return 4 * i + j


def turned(moves):
    other = [((3 - a, 3 - b), (3 - c, 3 - d)) for (a, b), (c, d) in moves]
    return [(number(*s), number(*t)) for s, t in moves + other]


def moves_of(kinds, target):
    grid = [(i, j) for i in range(4) for j in range(4) if i ^ j in kinds]
    return [(number(i, j), number(*target(i, j))) for i, j in grid]


LINE = turned(
    [
        ((2, 0), (2, 3)),
        ((2, 1), (3, 3)),
        ((3, 0), (2, 2)),
        ((3, 1), (3, 2)),
        ((2, 2), (2, 1)),
        ((3, 2), (3, 1)),
        ((2, 3), (2, 0)),
        ((3, 3), (3, 0)),
    ]
)
ACROSS = moves_of((0, 1, 2, 3), lambda i, j: (i ^ 2, j))
CORES = moves_of((0, 1, 2, 3), lambda i, j: (i ^ 1, j))
NEAR_DIAGONAL = moves_of((0, 2), lambda i, j: (i ^ 1, j ^ 1))
FAR_DIAGONAL = moves_of((2,), lambda i, j: (i ^ 1, j ^ 2))
LAST_DIAGONAL = moves_of((3,), lambda i, j: (i ^ 1, j ^ 1))


def send(array, moves):
    return lax.ppermute(array, AXES, moves)


def moved(names, moves):
    out = [None] * 16
    for source, target in moves:
        out[target] = names[source]
    return out


def whose_blocks():
    own = [(i, j) for i in range(4) for j in range(4)]
    kind = [i ^ j for i, j in own]
    line = moved(own, LINE)
    across = moved(own, ACROSS)
    line_across = moved(line, ACROSS)
    near = moved([own[d] if kind[d] == 0 else across[d] for d in range(16)], NEAR_DIAGONAL)
    far = moved(across, FAR_DIAGONAL)
    last = moved(line, LAST_DIAGONAL)
    diagonal = [(near, far, near, last)[kind[d]][d] for d in range(16)]
    mine = [own, across, line, line_across, diagonal]
    theirs = [moved(names, CORES) for names in mine]
    order = [own, theirs[0], across, theirs[1], line, theirs[2]]
    order += [line_across, diagonal, theirs[3], theirs[4]]
    table = np.array([[x[d] for x in order] for d in range(16)], np.int32)
    for d in range(16):
        assert len({tuple(sorted(ab)) for ab in table[d].tolist()}) == 10
    return table.reshape(16, 20)


def purify_kernel(where, *refs):
    blocks, patterns, out = refs[:10], refs[10:14], refs[14]
    full, mask, square, low, sems = refs[15:]
    edge = out.shape[0]
    order = full.shape[0]
    n = patterns[0].shape[0]
    step = edge // n
    i, j = where[20], where[21]

    def at(k):
        return pl.ds(pl.multiple_of(k * edge, 128), edge)

    def copy(k):
        a, b = where[2 * k], where[2 * k + 1]
        return pltpu.make_async_copy(blocks[k], full.at[at(a), at(b)], sems.at[k])

    for k in range(10):
        copy(k).start()
    r = lax.broadcasted_iota(jnp.int32, (n, edge), 0)
    c = lax.broadcasted_iota(jnp.int32, (n, edge), 1)
    widen = jnp.where(r == c // step, 1.0, 0.0).astype(BF16)
    for k, ref in enumerate(patterns):
        rows = jnp.dot(ref[...].astype(BF16), widen, preferred_element_type=F32)
        tall = jnp.broadcast_to(rows[:, None, :], (n, step, edge)).reshape(edge, edge)
        mask[:, at(jnp.bitwise_xor(j, k))] = tall
    for k in range(10):
        a, b = where[2 * k], where[2 * k + 1]
        copy(k).wait()

        @pl.when(a != b)
        def _():
            full[at(b), at(a)] = full[at(a), at(b)].T

    panel = full[at(i)]
    width = 256
    for t in range(order // width):
        cols = slice(t * width, (t + 1) * width)
        s = jnp.dot(panel, full[:, cols], preferred_element_type=F32) * mask[:, cols]
        square[:, cols] = s
        low[:, cols] = s.astype(BF16)
    cube = jnp.dot(low[...], full[:, at(j)], preferred_element_type=F32) * mask[:, at(j)]
    out[...] = (3.0 * square[:, at(j)] - 2.0 * cube).astype(BF16)


def block_body(own, pattern):
    edge = own.shape[0]
    order = 4 * edge
    i, j = lax.axis_index("wide"), lax.axis_index("narrow")
    kind = jnp.bitwise_xor(i, j)
    hold = lax.optimization_barrier
    line, across = send(own, LINE), send(own, ACROSS)
    near = send(jnp.where(kind == 0, own, across), NEAR_DIAGONAL)
    far = send(across, FAR_DIAGONAL)
    own_c, across_c = send(own, CORES), send(across, CORES)
    line, near, own_c, across_c = hold((line, near, own_c, across_c))
    line_across, last = send(line, ACROSS), send(line, LAST_DIAGONAL)
    pattern, line = hold((pattern, line))
    patterns = [pattern]
    for k in (1, 2, 3):
        patterns.append(lax.ppermute(pattern, "narrow", [(c, c ^ k) for c in range(4)]))
    line_across, last, far, patterns = hold((line_across, last, far, patterns))
    diagonal = jnp.where(kind == 3, last, jnp.where(kind == 1, far, near))
    line_c = send(line, CORES)
    line_across_c, diagonal_c = send(line_across, CORES), send(diagonal, CORES)
    table = jnp.asarray(whose_blocks())
    where = jnp.concatenate([table[number(i, j)], jnp.stack([i, j]).astype(jnp.int32)])
    vmem = pl.BlockSpec(memory_space=pltpu.VMEM)
    anywhere = pl.BlockSpec(memory_space=pl.ANY)
    return pl.pallas_call(
        purify_kernel,
        out_shape=jax.ShapeDtypeStruct((edge, edge), BF16),
        in_specs=[pl.BlockSpec(memory_space=pltpu.SMEM)] + [anywhere] * 10 + [vmem] * 4,
        out_specs=vmem,
        scratch_shapes=[
            pltpu.VMEM((order, order), BF16),
            pltpu.VMEM((edge, order), F32),
            pltpu.VMEM((edge, order), F32),
            pltpu.VMEM((edge, order), BF16),
            pltpu.SemaphoreType.DMA((10,)),
        ],
        compiler_params=pltpu.CompilerParams(vmem_limit_bytes=40 << 20),
        name="purify",
    )(
        where,
        *(own, own_c, across, across_c, line, line_c),
        *(line_across, diagonal, line_across_c, diagonal_c),
        *patterns,
    )


def solution(mesh):
    four = mesh.shape["wide"] == 4 and mesh.shape["narrow"] == 4

    def body(density, pattern):
        rows, cols = density.shape
        fits = rows == cols and rows % 128 == 0 and rows <= 512
        fits = fits and pattern.shape[0] == pattern.shape[1] <= 16
        return (block_body if four and fits else panel_body)(density, pattern)

    return jax.shard_map(
        body,
        mesh=mesh,
        in_specs=(P(("groups", "wide"), "narrow"), P(("groups", "wide"), "narrow")),
        out_specs=P(("groups", "wide"), "narrow"),
        check_vma=False,
    )
```

```python
import jax
import jax.numpy as jnp
from jax import lax
from jax.experimental import pallas as pl
from jax.experimental.pallas import tpu as pltpu
from jax.sharding import PartitionSpec as P

AXES = ("wide", "narrow")
F32, BF16 = jnp.float32, jnp.bfloat16


def expand(pattern, row_count, col_count):
    block_rows, block_cols = pattern.shape
    block_edge = row_count // block_rows
    spread_out = jnp.broadcast_to(
        pattern[:, None, :, None], (block_rows, block_edge, block_cols, block_edge)
    )
    return spread_out.reshape(row_count, col_count).astype(jnp.float32)


def panel_body(density, pattern):
    row_count, col_count = density.shape
    tile_mask = expand(pattern, row_count, col_count)
    row_panel = lax.all_gather(density, "narrow", axis=1, tiled=True)
    col_panel = lax.all_gather(density, "wide", axis=0, tiled=True)
    square = jnp.dot(row_panel, col_panel, preferred_element_type=F32) * tile_mask
    square_low = square.astype(BF16)
    square_panel = lax.all_gather(square_low, "narrow", axis=1, tiled=True)
    cube_sum = jnp.dot(square_panel, col_panel, preferred_element_type=F32) * tile_mask
    return (3.0 * square - 2.0 * cube_sum).astype(BF16)


def number(i, j):
    return 4 * i + j


def turned(moves):
    other = [((3 - a, 3 - b), (3 - c, 3 - d)) for (a, b), (c, d) in moves]
    return [(number(*s), number(*t)) for s, t in moves + other]


def moves_of(kinds, target):
    grid = [(i, j) for i in range(4) for j in range(4) if i ^ j in kinds]
    return [(number(i, j), number(*target(i, j))) for i, j in grid]


LINE = turned(
    [
        ((2, 0), (2, 3)),
        ((2, 1), (3, 3)),
        ((3, 0), (2, 2)),
        ((3, 1), (3, 2)),
        ((2, 2), (2, 1)),
        ((3, 2), (3, 1)),
        ((2, 3), (2, 0)),
        ((3, 3), (3, 0)),
    ]
)
ACROSS = moves_of((0, 1, 2, 3), lambda i, j: (i ^ 2, j))
CORES = moves_of((0, 1, 2, 3), lambda i, j: (i ^ 1, j))
NEAR_DIAGONAL = moves_of((0, 2), lambda i, j: (i ^ 1, j ^ 1))
FAR_DIAGONAL = moves_of((2,), lambda i, j: (i ^ 1, j ^ 2))
LAST_DIAGONAL = moves_of((3,), lambda i, j: (i ^ 1, j ^ 1))


def send(array, moves):
    return lax.ppermute(array, AXES, moves)


def moved(names, moves):
    out = [None] * 16
    for source, target in moves:
        out[target] = names[source]
    return out


def whose_blocks():
    own = [(i, j) for i in range(4) for j in range(4)]
    kind = [i ^ j for i, j in own]
    line = moved(own, LINE)
    across = moved(own, ACROSS)
    line_across = moved(line, ACROSS)
    near = moved([own[d] if kind[d] == 0 else across[d] for d in range(16)], NEAR_DIAGONAL)
    far = moved(across, FAR_DIAGONAL)
    last = moved(line, LAST_DIAGONAL)
    diagonal = [(near, far, near, last)[kind[d]][d] for d in range(16)]
    mine = [own, across, line, line_across, diagonal]
    theirs = [moved(names, CORES) for names in mine]
    order = [own, theirs[0], across, theirs[1], line, theirs[2]]
    order += [line_across, diagonal, theirs[3], theirs[4]]
    for d in range(16):
        assert len({tuple(sorted(names[d])) for names in order}) == 10
    return order


def spots(first, count, me):
    order = whose_blocks()[first : first + count]
    codes = [sum((4 * names[d][0] + names[d][1]) << 4 * k for k, names in enumerate(order)) for d in range(16)]
    code = jnp.int32(codes[0])
    for d in range(1, 16):
        code = jnp.where(me == d, codes[d], code)
    places = [jnp.bitwise_and(jnp.right_shift(code, 4 * k), 15) for k in range(count)]
    return [(jnp.right_shift(p, 2), jnp.bitwise_and(p, 3)) for p in places]


def block_at(edge, k):
    return pl.ds(pl.multiple_of(k * edge, 128), edge)


def place(first, blocks, full, sems):
    edge = blocks[0].shape[0]
    me = number(lax.axis_index("wide"), lax.axis_index("narrow"))
    copies = []
    for k, (a, b) in enumerate(spots(first, len(blocks), me)):
        spot, image = (block_at(edge, a), block_at(edge, b)), (block_at(edge, b), block_at(edge, a))
        copy = pltpu.make_async_copy(blocks[k], full.at[spot], sems.at[k])
        copies.append((copy, a != b, spot, image))
    for copy, *_ in copies:
        copy.start()
    return copies


def mirror(copies, full):
    for copy, off_diagonal, spot, image in copies:
        copy.wait()

        @pl.when(off_diagonal)
        def _():
            full[image] = full[spot].T


def early_kernel(*refs):
    blocks, full, sems = refs[:6], *refs[6:]
    mirror(place(0, blocks, full, sems), full)


def purify_kernel(full_in, *refs):
    blocks, patterns = refs[:4], refs[4:8]
    out, full, square, low, small, rows, sems = refs[8:]
    edge = out.shape[0]
    order = full.shape[0]
    n = small.shape[1]
    step = edge // n
    loads = [pltpu.make_async_copy(p, small.at[k], sems.at[4 + k]) for k, p in enumerate(patterns)]
    for load in loads:
        load.start()
    copies = place(6, blocks, full, sems)
    i, j = lax.axis_index("wide"), lax.axis_index("narrow")
    r = lax.broadcasted_iota(jnp.int32, (n, edge), 0)
    c = lax.broadcasted_iota(jnp.int32, (n, edge), 1)
    widen = jnp.where(r == c // step, 1.0, 0.0).astype(BF16)
    for k, load in enumerate(loads):
        load.wait()
        wide = jnp.dot(small[k].astype(BF16), widen, preferred_element_type=F32)
        rows[:, block_at(edge, jnp.bitwise_xor(j, k))] = wide
    mirror(copies, full)

    def masked(x, cols):
        tall = x.reshape(n, step, x.shape[1]) * rows[:, cols][:, None, :]
        return tall.reshape(x.shape)

    panel = full[block_at(edge, i)]
    width = 256
    for t in range(order // width):
        cols = slice(t * width, (t + 1) * width)
        s = masked(jnp.dot(panel, full[:, cols], preferred_element_type=F32), cols)
        square[:, cols] = s
        low[:, cols] = s.astype(BF16)
    mine = block_at(edge, j)
    cube = masked(jnp.dot(low[...], full[:, mine], preferred_element_type=F32), mine)
    out[...] = (3.0 * square[:, mine] - 2.0 * cube).astype(BF16)


VMEM = pl.BlockSpec(memory_space=pltpu.VMEM)
HBM = pl.BlockSpec(memory_space=pl.ANY)
PARAMS = pltpu.CompilerParams(vmem_limit_bytes=24 << 20)


def in_hbm(array):
    return pltpu.with_memory_space_constraint(array, pltpu.HBM)


def early(blocks):
    order = 4 * blocks[0].shape[0]
    return pl.pallas_call(
        early_kernel,
        out_shape=pltpu.VMEM((order, order), BF16),
        in_specs=[HBM] * 6,
        out_specs=VMEM,
        scratch_shapes=[pltpu.SemaphoreType.DMA((6,))],
        compiler_params=PARAMS,
        name="early",
    )(*blocks)


def purify(full, blocks, patterns):
    order = full.shape[0]
    edge = order // 4
    n = patterns[0].shape[0]
    full = pltpu.with_memory_space_constraint(full, pltpu.VMEM)
    return pl.pallas_call(
        purify_kernel,
        out_shape=(jax.ShapeDtypeStruct((edge, edge), BF16), pltpu.VMEM((order, order), BF16)),
        in_specs=[VMEM] + [HBM] * 8,
        out_specs=(VMEM, VMEM),
        input_output_aliases={0: 1},
        scratch_shapes=[
            pltpu.VMEM((edge, order), F32),
            pltpu.VMEM((edge, order), BF16),
            pltpu.VMEM((4, n, n), jnp.int32),
            pltpu.VMEM((n, order), F32),
            pltpu.SemaphoreType.DMA((8,)),
        ],
        compiler_params=PARAMS,
        name="purify",
    )(full, *blocks, *patterns)[0]


def block_body(own, pattern):
    i, j = lax.axis_index("wide"), lax.axis_index("narrow")
    kind = jnp.bitwise_xor(i, j)
    hold = lax.optimization_barrier
    line, across = send(own, LINE), send(own, ACROSS)
    near = send(jnp.where(kind == 0, own, across), NEAR_DIAGONAL)
    far = send(across, FAR_DIAGONAL)
    own_c, across_c = send(own, CORES), send(across, CORES)
    own_c, across_c, line = hold((own_c, across_c, line))
    line_across, last = send(line, ACROSS), send(line, LAST_DIAGONAL)
    line_c = send(line, CORES)
    pattern, line = hold((pattern, line))
    patterns = [pattern]
    for k in (1, 2, 3):
        patterns.append(lax.ppermute(pattern, "narrow", [(c, c ^ k) for c in range(4)]))
    full = early((own, own_c, across, across_c, line, line_c))
    patterns, near, far, last, line_across, full = hold((patterns, near, far, last, line_across, full))
    diagonal = jnp.where(kind == 3, last, jnp.where(kind == 1, far, near))
    line_across_c, diagonal_c = send(line_across, CORES), send(diagonal, CORES)
    blocks = (line_across, diagonal, line_across_c, diagonal_c)
    return purify(full, blocks, patterns)


def solution(mesh):
    four = mesh.shape["wide"] == 4 and mesh.shape["narrow"] == 4

    def body(density, pattern):
        rows, cols = density.shape
        fits = rows == cols and rows % 128 == 0 and rows <= 512
        fits = fits and pattern.shape[0] == pattern.shape[1] <= 16
        return (block_body if four and fits else panel_body)(density, pattern)

    return jax.shard_map(
        body,
        mesh=mesh,
        in_specs=(P(("groups", "wide"), "narrow"), P(("groups", "wide"), "narrow")),
        out_specs=P(("groups", "wide"), "narrow"),
        check_vma=False,
    )
```

```python
import jax
import jax.numpy as jnp
from jax import lax
from jax.experimental import pallas as pl
from jax.experimental.pallas import tpu as pltpu
from jax.sharding import PartitionSpec as P

AXES = ("wide", "narrow")
F32, BF16 = jnp.float32, jnp.bfloat16


def expand(pattern, row_count, col_count):
    block_rows, block_cols = pattern.shape
    block_edge = row_count // block_rows
    spread_out = jnp.broadcast_to(
        pattern[:, None, :, None], (block_rows, block_edge, block_cols, block_edge)
    )
    return spread_out.reshape(row_count, col_count).astype(jnp.float32)


def panel_body(density, pattern):
    row_count, col_count = density.shape
    tile_mask = expand(pattern, row_count, col_count)
    row_panel = lax.all_gather(density, "narrow", axis=1, tiled=True)
    col_panel = lax.all_gather(density, "wide", axis=0, tiled=True)
    square = jnp.dot(row_panel, col_panel, preferred_element_type=F32) * tile_mask
    square_low = square.astype(BF16)
    square_panel = lax.all_gather(square_low, "narrow", axis=1, tiled=True)
    cube_sum = jnp.dot(square_panel, col_panel, preferred_element_type=F32) * tile_mask
    return (3.0 * square - 2.0 * cube_sum).astype(BF16)


def number(i, j):
    return 4 * i + j


def turned(moves):
    other = [((3 - a, 3 - b), (3 - c, 3 - d)) for (a, b), (c, d) in moves]
    return [(number(*s), number(*t)) for s, t in moves + other]


def moves_of(kinds, target):
    grid = [(i, j) for i in range(4) for j in range(4) if i ^ j in kinds]
    return [(number(i, j), number(*target(i, j))) for i, j in grid]


LINE = turned(
    [
        ((2, 0), (2, 3)),
        ((2, 1), (3, 3)),
        ((3, 0), (2, 2)),
        ((3, 1), (3, 2)),
        ((2, 2), (2, 1)),
        ((3, 2), (3, 1)),
        ((2, 3), (2, 0)),
        ((3, 3), (3, 0)),
    ]
)
ACROSS = moves_of((0, 1, 2, 3), lambda i, j: (i ^ 2, j))
CORES = moves_of((0, 1, 2, 3), lambda i, j: (i ^ 1, j))
NEAR_DIAGONAL = moves_of((0, 2), lambda i, j: (i ^ 1, j ^ 1))
FAR_DIAGONAL = moves_of((2,), lambda i, j: (i ^ 1, j ^ 2))
LAST_DIAGONAL = moves_of((3,), lambda i, j: (i ^ 1, j ^ 1))


def send(array, moves):
    return lax.ppermute(array, AXES, moves)


def moved(names, moves):
    out = [None] * 16
    for source, target in moves:
        out[target] = names[source]
    return out


def whose_blocks():
    own = [(i, j) for i in range(4) for j in range(4)]
    kind = [i ^ j for i, j in own]
    line = moved(own, LINE)
    across = moved(own, ACROSS)
    line_across = moved(line, ACROSS)
    near = moved([own[d] if kind[d] == 0 else across[d] for d in range(16)], NEAR_DIAGONAL)
    far = moved(across, FAR_DIAGONAL)
    last = moved(line, LAST_DIAGONAL)
    diagonal = [(near, far, near, last)[kind[d]][d] for d in range(16)]
    mine = [own, across, line, line_across, diagonal]
    theirs = [moved(names, CORES) for names in mine]
    order = [own, theirs[0], across, theirs[1], line, theirs[2], line_across, diagonal, theirs[3], theirs[4]]
    for d in range(16):
        assert len({tuple(sorted(names[d])) for names in order}) == 10
    return order


def spots(first, count, me):
    order = whose_blocks()[first : first + count]
    codes = [sum((4 * names[d][0] + names[d][1]) << 4 * k for k, names in enumerate(order)) for d in range(16)]
    code = jnp.int32(codes[0])
    for d in range(1, 16):
        code = jnp.where(me == d, codes[d], code)
    places = [jnp.bitwise_and(jnp.right_shift(code, 4 * k), 15) for k in range(count)]
    return [(jnp.right_shift(p, 2), jnp.bitwise_and(p, 3)) for p in places]


def block_at(edge, k):
    return pl.ds(pl.multiple_of(k * edge, 128), edge)


def place(first, blocks, full, sems):
    edge = blocks[0].shape[0]
    me = number(lax.axis_index("wide"), lax.axis_index("narrow"))
    copies = []
    for k, (a, b) in enumerate(spots(first, len(blocks), me)):
        spot, image = (block_at(edge, a), block_at(edge, b)), (block_at(edge, b), block_at(edge, a))
        copy = pltpu.make_async_copy(blocks[k], full.at[spot], sems.at[k])
        copies.append((copy, a != b, spot, image))
    for copy, *_ in copies:
        copy.start()
    return copies


def mirror(copies, full):
    for copy, off_diagonal, spot, image in copies:
        copy.wait()

        @pl.when(off_diagonal)
        def _():
            full[image] = full[spot].T


def early_kernel(*refs):
    blocks, full, sems = refs[:-2], *refs[-2:]
    mirror(place(0, blocks, full, sems), full)


def purify_kernel(full_in, *refs):
    blocks, patterns = refs[:-11], refs[-11:-7]
    out, full, square, low, small, rows, sems = refs[-7:]
    late = len(blocks)
    edge = out.shape[0]
    order = full.shape[0]
    n = small.shape[1]
    step = edge // n
    loads = [pltpu.make_async_copy(p, small.at[k], sems.at[late + k]) for k, p in enumerate(patterns)]
    for load in loads:
        load.start()
    copies = place(10 - late, blocks, full, sems)
    i, j = lax.axis_index("wide"), lax.axis_index("narrow")
    r = lax.broadcasted_iota(jnp.int32, (n, edge), 0)
    c = lax.broadcasted_iota(jnp.int32, (n, edge), 1)
    widen = jnp.where(r == c // step, 1.0, 0.0).astype(BF16)
    for k, load in enumerate(loads):
        load.wait()
        wide = jnp.dot(small[k].astype(BF16), widen, preferred_element_type=F32)
        rows[:, block_at(edge, jnp.bitwise_xor(j, k))] = wide
    mirror(copies, full)

    def masked(x, cols):
        tall = x.reshape(n, step, x.shape[1]) * rows[:, cols][:, None, :]
        return tall.reshape(x.shape)

    panel = full[block_at(edge, i)]
    width = 256
    for t in range(order // width):
        cols = slice(t * width, (t + 1) * width)
        s = masked(jnp.dot(panel, full[:, cols], preferred_element_type=F32), cols)
        square[:, cols] = s
        low[:, cols] = s.astype(BF16)
    mine = block_at(edge, j)
    cube = masked(jnp.dot(low[...], full[:, mine], preferred_element_type=F32), mine)
    out[...] = (3.0 * square[:, mine] - 2.0 * cube).astype(BF16)


VMEM = pl.BlockSpec(memory_space=pltpu.VMEM)
HBM = pl.BlockSpec(memory_space=pl.ANY)
PARAMS = pltpu.CompilerParams(vmem_limit_bytes=24 << 20)


def in_hbm(array):
    return pltpu.with_memory_space_constraint(array, pltpu.HBM)


def early(blocks):
    order = 4 * blocks[0].shape[0]
    return pl.pallas_call(
        early_kernel,
        out_shape=pltpu.VMEM((order, order), BF16),
        in_specs=[HBM] * len(blocks),
        out_specs=VMEM,
        scratch_shapes=[pltpu.SemaphoreType.DMA((len(blocks),))],
        compiler_params=PARAMS,
        name="early",
    )(*blocks)


def purify(full, blocks, patterns):
    order = full.shape[0]
    edge = order // 4
    n = patterns[0].shape[0]
    full = pltpu.with_memory_space_constraint(full, pltpu.VMEM)
    return pl.pallas_call(
        purify_kernel,
        out_shape=(jax.ShapeDtypeStruct((edge, edge), BF16), pltpu.VMEM((order, order), BF16)),
        in_specs=[VMEM] + [HBM] * (len(blocks) + 4),
        out_specs=(VMEM, VMEM),
        input_output_aliases={0: 1},
        scratch_shapes=[
            pltpu.VMEM((edge, order), F32),
            pltpu.VMEM((edge, order), BF16),
            pltpu.VMEM((4, n, n), jnp.int32),
            pltpu.VMEM((n, order), F32),
            pltpu.SemaphoreType.DMA((len(blocks) + 4,)),
        ],
        compiler_params=PARAMS,
        name="purify",
    )(full, *blocks, *patterns)[0]


def block_body(own, pattern):
    i, j = lax.axis_index("wide"), lax.axis_index("narrow")
    kind = jnp.bitwise_xor(i, j)
    hold = lax.optimization_barrier
    line, across = send(own, LINE), send(own, ACROSS)
    near = send(jnp.where(kind == 0, own, across), NEAR_DIAGONAL)
    far = send(across, FAR_DIAGONAL)
    own_c, across_c = send(own, CORES), send(across, CORES)
    own_c, across_c, line = hold((own_c, across_c, line))
    line_across, last = send(line, ACROSS), send(line, LAST_DIAGONAL)
    line_c = send(line, CORES)
    pattern, line = hold((pattern, line))
    got = {k: lax.ppermute(pattern, "narrow", [(c, c ^ k) for c in range(4)]) for k in (1, 2, 3)}
    patterns = [pattern, got[1], got[2], got[3]]
    full = early((own, own_c, across, across_c, line, line_c,))
    patterns, full = hold((patterns, full))
    line_across, full = hold((line_across, full))
    line_across_c = send(line_across, CORES)
    diagonal = jnp.where(kind == 3, last, jnp.where(kind == 1, far, near))
    diagonal_c = send(diagonal, CORES)
    blocks = (line_across, diagonal, line_across_c, diagonal_c)
    return purify(full, blocks, patterns)


def solution(mesh):
    four = mesh.shape["wide"] == 4 and mesh.shape["narrow"] == 4

    def body(density, pattern):
        rows, cols = density.shape
        fits = rows == cols and rows % 128 == 0 and rows <= 512
        fits = fits and pattern.shape[0] == pattern.shape[1] <= 16
        return (block_body if four and fits else panel_body)(density, pattern)

    return jax.shard_map(
        body,
        mesh=mesh,
        in_specs=(P(("groups", "wide"), "narrow"), P(("groups", "wide"), "narrow")),
        out_specs=P(("groups", "wide"), "narrow"),
        check_vma=False,
    )
```

```python
import jax
import jax.numpy as jnp
from jax import lax
from jax.experimental import pallas as pl
from jax.experimental.pallas import tpu as pltpu
from jax.sharding import PartitionSpec as P

AXES = ("wide", "narrow")
F32, BF16 = jnp.float32, jnp.bfloat16


def expand(pattern, row_count, col_count):
    block_rows, block_cols = pattern.shape
    block_edge = row_count // block_rows
    spread_out = jnp.broadcast_to(
        pattern[:, None, :, None], (block_rows, block_edge, block_cols, block_edge)
    )
    return spread_out.reshape(row_count, col_count).astype(jnp.float32)


def panel_body(density, pattern):
    row_count, col_count = density.shape
    tile_mask = expand(pattern, row_count, col_count)
    row_panel = lax.all_gather(density, "narrow", axis=1, tiled=True)
    col_panel = lax.all_gather(density, "wide", axis=0, tiled=True)
    square = jnp.dot(row_panel, col_panel, preferred_element_type=F32) * tile_mask
    square_low = square.astype(BF16)
    square_panel = lax.all_gather(square_low, "narrow", axis=1, tiled=True)
    cube_sum = jnp.dot(square_panel, col_panel, preferred_element_type=F32) * tile_mask
    return (3.0 * square - 2.0 * cube_sum).astype(BF16)


def number(i, j):
    return 4 * i + j


def turned(moves):
    other = [((3 - a, 3 - b), (3 - c, 3 - d)) for (a, b), (c, d) in moves]
    return [(number(*s), number(*t)) for s, t in moves + other]


def moves_of(kinds, target):
    grid = [(i, j) for i in range(4) for j in range(4) if i ^ j in kinds]
    return [(number(i, j), number(*target(i, j))) for i, j in grid]


LINE = turned(
    [
        ((2, 0), (2, 3)),
        ((2, 1), (3, 3)),
        ((3, 0), (2, 2)),
        ((3, 1), (3, 2)),
        ((2, 2), (2, 1)),
        ((3, 2), (3, 1)),
        ((2, 3), (2, 0)),
        ((3, 3), (3, 0)),
    ]
)
ACROSS = moves_of((0, 1, 2, 3), lambda i, j: (i ^ 2, j))
CORES = moves_of((0, 1, 2, 3), lambda i, j: (i ^ 1, j))
NEAR_DIAGONAL = moves_of((0, 2), lambda i, j: (i ^ 1, j ^ 1))
FAR_DIAGONAL = moves_of((2,), lambda i, j: (i ^ 1, j ^ 2))
LAST_DIAGONAL = moves_of((3,), lambda i, j: (i ^ 1, j ^ 1))


def send(array, moves):
    return lax.ppermute(array, AXES, moves)


def moved(names, moves):
    out = [None] * 16
    for source, target in moves:
        out[target] = names[source]
    return out


def whose_blocks():
    own = [(i, j) for i in range(4) for j in range(4)]
    kind = [i ^ j for i, j in own]
    line = moved(own, LINE)
    across = moved(own, ACROSS)
    line_across = moved(line, ACROSS)
    near = moved([own[d] if kind[d] == 0 else across[d] for d in range(16)], NEAR_DIAGONAL)
    far = moved(across, FAR_DIAGONAL)
    last = moved(line, LAST_DIAGONAL)
    diagonal = [(near, far, near, last)[kind[d]][d] for d in range(16)]
    mine = [own, across, line, line_across, diagonal]
    theirs = [moved(names, CORES) for names in mine]
    order = [own, theirs[0], across, theirs[1], line, theirs[2]]
    order += [line_across, diagonal, theirs[4], theirs[3]]
    for d in range(16):
        assert len({tuple(sorted(names[d])) for names in order}) == 10
    return order


def spots(first, count, me):
    order = whose_blocks()[first : first + count]
    codes = [sum((4 * names[d][0] + names[d][1]) << 4 * k for k, names in enumerate(order)) for d in range(16)]
    code = jnp.int32(codes[0])
    for d in range(1, 16):
        code = jnp.where(me == d, codes[d], code)
    places = [jnp.bitwise_and(jnp.right_shift(code, 4 * k), 15) for k in range(count)]
    return [(jnp.right_shift(p, 2), jnp.bitwise_and(p, 3)) for p in places]


def block_at(edge, k):
    return pl.ds(pl.multiple_of(k * edge, 128), edge)


def place(first, blocks, full, sems):
    edge = blocks[0].shape[0]
    me = number(lax.axis_index("wide"), lax.axis_index("narrow"))
    copies = []
    for k, (a, b) in enumerate(spots(first, len(blocks), me)):
        spot, image = (block_at(edge, a), block_at(edge, b)), (block_at(edge, b), block_at(edge, a))
        copy = pltpu.make_async_copy(blocks[k], full.at[spot], sems.at[k])
        copies.append((copy, a != b, spot, image))
    for copy, *_ in copies:
        copy.start()
    return copies


def mirror(copies, full):
    for copy, off_diagonal, spot, image in copies:
        copy.wait()

        @pl.when(off_diagonal)
        def _():
            full[image] = full[spot].T


def early_kernel(*refs):
    blocks, full, sems = refs[:-2], *refs[-2:]
    mirror(place(0, blocks, full, sems), full)


def middle_kernel(full_in, *refs):
    blocks, patterns, (full, rows, small, sems) = refs[:-8], refs[-8:-4], refs[-4:]
    edge = blocks[0].shape[0]
    n = small.shape[1]
    step = edge // n
    count = len(blocks)
    loads = [pltpu.make_async_copy(p, small.at[k], sems.at[count + k]) for k, p in enumerate(patterns)]
    for load in loads:
        load.start()
    copies = place(6, blocks, full, sems)
    j = lax.axis_index("narrow")
    r = lax.broadcasted_iota(jnp.int32, (n, edge), 0)
    c = lax.broadcasted_iota(jnp.int32, (n, edge), 1)
    widen = jnp.where(r == c // step, 1.0, 0.0).astype(BF16)
    for k, load in enumerate(loads):
        load.wait()
        wide = jnp.dot(small[k].astype(BF16), widen, preferred_element_type=F32)
        rows[:, block_at(edge, jnp.bitwise_xor(j, k))] = wide
    mirror(copies, full)


def purify_kernel(full_in, rows, *refs):
    blocks, (out, full, square, low, sems) = refs[:-5], refs[-5:]
    edge = out.shape[0]
    order = full.shape[0]
    n = rows.shape[0]
    step = edge // n
    mirror(place(10 - len(blocks), blocks, full, sems), full)
    i, j = lax.axis_index("wide"), lax.axis_index("narrow")

    def masked(x, cols):
        tall = x.reshape(n, step, x.shape[1]) * rows[:, cols][:, None, :]
        return tall.reshape(x.shape)

    panel = full[block_at(edge, i)]
    width = 256
    for t in range(order // width):
        cols = slice(t * width, (t + 1) * width)
        s = masked(jnp.dot(panel, full[:, cols], preferred_element_type=F32), cols)
        square[:, cols] = s
        low[:, cols] = s.astype(BF16)
    mine = block_at(edge, j)
    cube = masked(jnp.dot(low[...], full[:, mine], preferred_element_type=F32), mine)
    out[...] = (3.0 * square[:, mine] - 2.0 * cube).astype(BF16)


VMEM = pl.BlockSpec(memory_space=pltpu.VMEM)
HBM = pl.BlockSpec(memory_space=pl.ANY)
PARAMS = pltpu.CompilerParams(vmem_limit_bytes=24 << 20)


def in_vmem(array):
    return pltpu.with_memory_space_constraint(array, pltpu.VMEM)


def early(blocks):
    order = 4 * blocks[0].shape[0]
    return pl.pallas_call(
        early_kernel,
        out_shape=pltpu.VMEM((order, order), BF16),
        in_specs=[HBM] * len(blocks),
        out_specs=VMEM,
        scratch_shapes=[pltpu.SemaphoreType.DMA((len(blocks),))],
        compiler_params=PARAMS,
        name="early",
    )(*blocks)


def middle(full, blocks, patterns):
    order = full.shape[0]
    n = patterns[0].shape[0]
    return pl.pallas_call(
        middle_kernel,
        out_shape=(pltpu.VMEM((order, order), BF16), pltpu.VMEM((n, order), F32)),
        in_specs=[VMEM] + [HBM] * (len(blocks) + 4),
        out_specs=(VMEM, VMEM),
        input_output_aliases={0: 0},
        scratch_shapes=[
            pltpu.VMEM((4, n, n), jnp.int32),
            pltpu.SemaphoreType.DMA((len(blocks) + 4,)),
        ],
        compiler_params=PARAMS,
        name="middle",
    )(in_vmem(full), *blocks, *patterns)


def purify(full, rows, blocks):
    order = full.shape[0]
    edge = order // 4
    return pl.pallas_call(
        purify_kernel,
        out_shape=(jax.ShapeDtypeStruct((edge, edge), BF16), pltpu.VMEM((order, order), BF16)),
        in_specs=[VMEM, VMEM] + [HBM] * len(blocks),
        out_specs=(VMEM, VMEM),
        input_output_aliases={0: 1},
        scratch_shapes=[
            pltpu.VMEM((edge, order), F32),
            pltpu.VMEM((edge, order), BF16),
            pltpu.SemaphoreType.DMA((len(blocks),)),
        ],
        compiler_params=PARAMS,
        name="purify",
    )(in_vmem(full), in_vmem(rows), *blocks)[0]


def block_body(own, pattern):
    i, j = lax.axis_index("wide"), lax.axis_index("narrow")
    kind = jnp.bitwise_xor(i, j)
    hold = lax.optimization_barrier
    line, across = send(own, LINE), send(own, ACROSS)
    near = send(jnp.where(kind == 0, own, across), NEAR_DIAGONAL)
    far = send(across, FAR_DIAGONAL)
    own_c, across_c = send(own, CORES), send(across, CORES)
    own_c, across_c, line = hold((own_c, across_c, line))
    line_across, last = send(line, ACROSS), send(line, LAST_DIAGONAL)
    line_c = send(line, CORES)
    pattern, line = hold((pattern, line))
    got = {k: lax.ppermute(pattern, "narrow", [(c, c ^ k) for c in range(4)]) for k in (1, 2, 3)}
    patterns = [pattern, got[1], got[2], got[3]]
    full = early((own, own_c, across, across_c, line, line_c,))
    patterns, full = hold((patterns, full))
    line_across, full = hold((line_across, full))
    line_across_c = send(line_across, CORES)
    diagonal = jnp.where(kind == 3, last, jnp.where(kind == 1, far, near))
    diagonal_c = send(diagonal, CORES)
    full, rows = middle(full, (line_across, diagonal, diagonal_c), patterns)
    return purify(full, rows, (line_across_c,))


def solution(mesh):
    four = mesh.shape["wide"] == 4 and mesh.shape["narrow"] == 4

    def body(density, pattern):
        rows, cols = density.shape
        fits = rows == cols and rows % 128 == 0 and rows <= 512
        fits = fits and pattern.shape[0] == pattern.shape[1] <= 16
        return (block_body if four and fits else panel_body)(density, pattern)

    return jax.shard_map(
        body,
        mesh=mesh,
        in_specs=(P(("groups", "wide"), "narrow"), P(("groups", "wide"), "narrow")),
        out_specs=P(("groups", "wide"), "narrow"),
        check_vma=False,
    )
```

```python
import jax
import jax.numpy as jnp
from jax import lax
from jax.experimental import pallas as pl
from jax.experimental.pallas import tpu as pltpu
from jax.sharding import PartitionSpec as P

AXES = ("wide", "narrow")
F32, BF16 = jnp.float32, jnp.bfloat16


def expand(pattern, row_count, col_count):
    block_rows, block_cols = pattern.shape
    block_edge = row_count // block_rows
    spread_out = jnp.broadcast_to(
        pattern[:, None, :, None], (block_rows, block_edge, block_cols, block_edge)
    )
    return spread_out.reshape(row_count, col_count).astype(jnp.float32)


def panel_body(density, pattern):
    row_count, col_count = density.shape
    tile_mask = expand(pattern, row_count, col_count)
    row_panel = lax.all_gather(density, "narrow", axis=1, tiled=True)
    col_panel = lax.all_gather(density, "wide", axis=0, tiled=True)
    square = jnp.dot(row_panel, col_panel, preferred_element_type=F32) * tile_mask
    square_low = square.astype(BF16)
    square_panel = lax.all_gather(square_low, "narrow", axis=1, tiled=True)
    cube_sum = jnp.dot(square_panel, col_panel, preferred_element_type=F32) * tile_mask
    return (3.0 * square - 2.0 * cube_sum).astype(BF16)


def number(i, j):
    return 4 * i + j


def turned(moves):
    other = [((3 - a, 3 - b), (3 - c, 3 - d)) for (a, b), (c, d) in moves]
    return [(number(*s), number(*t)) for s, t in moves + other]


def moves_of(kinds, target):
    grid = [(i, j) for i in range(4) for j in range(4) if i ^ j in kinds]
    return [(number(i, j), number(*target(i, j))) for i, j in grid]


LINE = turned(
    [
        ((2, 0), (2, 3)),
        ((2, 1), (3, 3)),
        ((3, 0), (2, 2)),
        ((3, 1), (3, 2)),
        ((2, 2), (2, 1)),
        ((3, 2), (3, 1)),
        ((2, 3), (2, 0)),
        ((3, 3), (3, 0)),
    ]
)
ACROSS = moves_of((0, 1, 2, 3), lambda i, j: (i ^ 2, j))
CORES = moves_of((0, 1, 2, 3), lambda i, j: (i ^ 1, j))
NEAR_DIAGONAL = moves_of((0, 2), lambda i, j: (i ^ 1, j ^ 1))
FAR_DIAGONAL = moves_of((2,), lambda i, j: (i ^ 1, j ^ 2))
LAST_DIAGONAL = moves_of((3,), lambda i, j: (i ^ 1, j ^ 1))


def send(array, moves):
    return lax.ppermute(array, AXES, moves)


def moved(names, moves):
    out = [None] * 16
    for source, target in moves:
        out[target] = names[source]
    return out


def whose_blocks():
    own = [(i, j) for i in range(4) for j in range(4)]
    kind = [i ^ j for i, j in own]
    line = moved(own, LINE)
    across = moved(own, ACROSS)
    line_across = moved(line, ACROSS)
    near = moved([own[d] if kind[d] == 0 else across[d] for d in range(16)], NEAR_DIAGONAL)
    far = moved(across, FAR_DIAGONAL)
    last = moved(line, LAST_DIAGONAL)
    diagonal = [(near, far, near, last)[kind[d]][d] for d in range(16)]
    mine = [own, across, line, line_across, diagonal]
    theirs = [moved(names, CORES) for names in mine]
    order = [own, theirs[0], across, theirs[1], line, theirs[2]]
    order += [line_across, diagonal, theirs[4], theirs[3]]
    for d in range(16):
        assert len({tuple(sorted(names[d])) for names in order}) == 10
    return order


def spots(first, count, me):
    order = whose_blocks()[first : first + count]
    codes = [sum((4 * names[d][0] + names[d][1]) << 4 * k for k, names in enumerate(order)) for d in range(16)]
    code = jnp.int32(codes[0])
    for d in range(1, 16):
        code = jnp.where(me == d, codes[d], code)
    places = [jnp.bitwise_and(jnp.right_shift(code, 4 * k), 15) for k in range(count)]
    return [(jnp.right_shift(p, 2), jnp.bitwise_and(p, 3)) for p in places]


def block_at(edge, k):
    return pl.ds(pl.multiple_of(k * edge, 128), edge)


def place(first, blocks, full, sems):
    edge = blocks[0].shape[0]
    me = number(lax.axis_index("wide"), lax.axis_index("narrow"))
    copies = []
    for k, (a, b) in enumerate(spots(first, len(blocks), me)):
        spot, image = (block_at(edge, a), block_at(edge, b)), (block_at(edge, b), block_at(edge, a))
        copy = pltpu.make_async_copy(blocks[k], full.at[spot], sems.at[k])
        copies.append((copy, a != b, spot, image))
    for copy, *_ in copies:
        copy.start()
    return copies


def mirror(copies, full):
    for copy, off_diagonal, spot, image in copies:
        copy.wait()

        @pl.when(off_diagonal)
        def _():
            full[image] = full[spot].T


def early_kernel(*refs):
    blocks, full, sems = refs[:-2], *refs[-2:]
    mirror(place(0, blocks, full, sems), full)


def square_columns(first, count, full, rows, square, low):
    n, edge = rows.shape[0], square.shape[0]
    panel = full[block_at(edge, lax.axis_index("wide"))]
    for t in range(count):
        cols = pl.ds(pl.multiple_of(first + 256 * t, 128), 256)
        s = jnp.dot(panel, full[:, cols], preferred_element_type=F32)
        s = masked(s, rows[:, cols])
        square[:, cols] = s
        low[:, cols] = s.astype(BF16)


def masked(x, rows):
    n = rows.shape[0]
    tall = x.reshape(n, x.shape[0] // n, x.shape[1]) * rows[:, None, :]
    return tall.reshape(x.shape)


def middle_kernel(full_in, *refs):
    blocks, patterns, (full, rows, square, low, small, sems) = refs[:-10], refs[-10:-6], refs[-6:]
    edge, order = square.shape
    n = small.shape[1]
    step = edge // n
    count = len(blocks)
    loads = [pltpu.make_async_copy(p, small.at[k], sems.at[count + k]) for k, p in enumerate(patterns)]
    for load in loads:
        load.start()
    copies = place(6, blocks, full, sems)
    i, j = lax.axis_index("wide"), lax.axis_index("narrow")
    r = lax.broadcasted_iota(jnp.int32, (n, edge), 0)
    c = lax.broadcasted_iota(jnp.int32, (n, edge), 1)
    widen = jnp.where(r == c // step, 1.0, 0.0).astype(BF16)
    for k, load in enumerate(loads):
        load.wait()
        wide = jnp.dot(small[k].astype(BF16), widen, preferred_element_type=F32)
        rows[:, block_at(edge, jnp.bitwise_xor(j, k))] = wide
    mirror(copies, full)

    @pl.when(jnp.right_shift(i, 1) == jnp.right_shift(j, 1))
    def _():
        square_columns(jnp.right_shift(i, 1) * (order // 2), order // 512, full, rows, square, low)


def purify_kernel(full_in, rows, square_in, low_in, *refs):
    blocks, (out, full, square, low, sems) = refs[:-5], refs[-5:]
    edge, order = square.shape
    mirror(place(10 - len(blocks), blocks, full, sems), full)
    i, j = lax.axis_index("wide"), lax.axis_index("narrow")
    half = jnp.right_shift(i, 1)

    @pl.when(half == jnp.right_shift(j, 1))
    def _():
        square_columns((1 - half) * (order // 2), order // 512, full, rows, square, low)

    @pl.when(half != jnp.right_shift(j, 1))
    def _():
        square_columns(0, order // 256, full, rows, square, low)

    mine = block_at(edge, j)
    cube = jnp.dot(low[...], full[:, mine], preferred_element_type=F32)
    cube = masked(cube, rows[:, mine])
    out[...] = (3.0 * square[:, mine] - 2.0 * cube).astype(BF16)


VMEM = pl.BlockSpec(memory_space=pltpu.VMEM)
HBM = pl.BlockSpec(memory_space=pl.ANY)
PARAMS = pltpu.CompilerParams(vmem_limit_bytes=24 << 20)


def in_vmem(array):
    return pltpu.with_memory_space_constraint(array, pltpu.VMEM)


def early(blocks):
    order = 4 * blocks[0].shape[0]
    return pl.pallas_call(
        early_kernel,
        out_shape=pltpu.VMEM((order, order), BF16),
        in_specs=[HBM] * len(blocks),
        out_specs=VMEM,
        scratch_shapes=[pltpu.SemaphoreType.DMA((len(blocks),))],
        compiler_params=PARAMS,
        name="early",
    )(*blocks)


def middle(full, blocks, patterns):
    order = full.shape[0]
    edge = order // 4
    n = patterns[0].shape[0]
    return pl.pallas_call(
        middle_kernel,
        out_shape=(
            pltpu.VMEM((order, order), BF16),
            pltpu.VMEM((n, order), F32),
            pltpu.VMEM((edge, order), F32),
            pltpu.VMEM((edge, order), BF16),
        ),
        in_specs=[VMEM] + [HBM] * (len(blocks) + 4),
        out_specs=(VMEM,) * 4,
        input_output_aliases={0: 0},
        scratch_shapes=[
            pltpu.VMEM((4, n, n), jnp.int32),
            pltpu.SemaphoreType.DMA((len(blocks) + 4,)),
        ],
        compiler_params=PARAMS,
        name="middle",
    )(in_vmem(full), *blocks, *patterns)


def purify(full, rows, square, low, blocks):
    edge, order = square.shape
    return pl.pallas_call(
        purify_kernel,
        out_shape=(
            jax.ShapeDtypeStruct((edge, edge), BF16),
            pltpu.VMEM((order, order), BF16),
            pltpu.VMEM((edge, order), F32),
            pltpu.VMEM((edge, order), BF16),
        ),
        in_specs=[VMEM] * 4 + [HBM] * len(blocks),
        out_specs=(VMEM,) * 4,
        input_output_aliases={0: 1, 2: 2, 3: 3},
        scratch_shapes=[pltpu.SemaphoreType.DMA((len(blocks),))],
        compiler_params=PARAMS,
        name="purify",
    )(*map(in_vmem, (full, rows, square, low)), *blocks)[0]


def block_body(own, pattern):
    i, j = lax.axis_index("wide"), lax.axis_index("narrow")
    kind = jnp.bitwise_xor(i, j)
    hold = lax.optimization_barrier
    line, across = send(own, LINE), send(own, ACROSS)
    near = send(jnp.where(kind == 0, own, across), NEAR_DIAGONAL)
    far = send(across, FAR_DIAGONAL)
    own_c, across_c = send(own, CORES), send(across, CORES)
    own_c, across_c, line = hold((own_c, across_c, line))
    line_across, last = send(line, ACROSS), send(line, LAST_DIAGONAL)
    line_c = send(line, CORES)
    pattern, line = hold((pattern, line))
    got = {k: lax.ppermute(pattern, "narrow", [(c, c ^ k) for c in range(4)]) for k in (1, 2, 3)}
    patterns = [pattern, got[1], got[2], got[3]]
    full = early((own, own_c, across, across_c, line, line_c))
    patterns, full = hold((patterns, full))
    line_across, full = hold((line_across, full))
    line_across_c = send(line_across, CORES)
    diagonal = jnp.where(kind == 3, last, jnp.where(kind == 1, far, near))
    diagonal_c = send(diagonal, CORES)
    full, rows, square, low = middle(full, (line_across, diagonal, diagonal_c), patterns)
    return purify(full, rows, square, low, (line_across_c,))


def solution(mesh):
    four = mesh.shape["wide"] == 4 and mesh.shape["narrow"] == 4

    def body(density, pattern):
        rows, cols = density.shape
        fits = rows == cols and rows % 128 == 0 and rows <= 512
        fits = fits and pattern.shape[0] == pattern.shape[1] <= 16
        return (block_body if four and fits else panel_body)(density, pattern)

    return jax.shard_map(
        body,
        mesh=mesh,
        in_specs=(P(("groups", "wide"), "narrow"), P(("groups", "wide"), "narrow")),
        out_specs=P(("groups", "wide"), "narrow"),
        check_vma=False,
    )
```

```python
import jax
import jax.numpy as jnp
from jax import lax
from jax.experimental import pallas as pl
from jax.experimental.pallas import tpu as pltpu
from jax.sharding import PartitionSpec as P

AXES = ("wide", "narrow")
F32, BF16 = jnp.float32, jnp.bfloat16


def expand(pattern, row_count, col_count):
    block_rows, block_cols = pattern.shape
    block_edge = row_count // block_rows
    spread_out = jnp.broadcast_to(
        pattern[:, None, :, None], (block_rows, block_edge, block_cols, block_edge)
    )
    return spread_out.reshape(row_count, col_count).astype(jnp.float32)


def panel_body(density, pattern):
    row_count, col_count = density.shape
    tile_mask = expand(pattern, row_count, col_count)
    row_panel = lax.all_gather(density, "narrow", axis=1, tiled=True)
    col_panel = lax.all_gather(density, "wide", axis=0, tiled=True)
    square = jnp.dot(row_panel, col_panel, preferred_element_type=F32) * tile_mask
    square_low = square.astype(BF16)
    square_panel = lax.all_gather(square_low, "narrow", axis=1, tiled=True)
    cube_sum = jnp.dot(square_panel, col_panel, preferred_element_type=F32) * tile_mask
    return (3.0 * square - 2.0 * cube_sum).astype(BF16)


def number(i, j):
    return 4 * i + j


def turned(moves):
    other = [((3 - a, 3 - b), (3 - c, 3 - d)) for (a, b), (c, d) in moves]
    return [(number(*s), number(*t)) for s, t in moves + other]


def moves_of(kinds, target):
    grid = [(i, j) for i in range(4) for j in range(4) if i ^ j in kinds]
    return [(number(i, j), number(*target(i, j))) for i, j in grid]


LINE = turned(
    [
        ((2, 0), (3, 3)),
        ((2, 1), (2, 3)),
        ((3, 0), (2, 2)),
        ((3, 1), (3, 2)),
        ((2, 2), (2, 1)),
        ((3, 2), (3, 1)),
        ((2, 3), (2, 0)),
        ((3, 3), (3, 0)),
    ]
)
ACROSS = moves_of((0, 1, 2, 3), lambda i, j: (i ^ 2, j))
CORES = moves_of((0, 1, 2, 3), lambda i, j: (i ^ 1, j))
NEAR_DIAGONAL = moves_of((0, 2), lambda i, j: (i ^ 1, j ^ 1))
FAR_DIAGONAL = moves_of((2,), lambda i, j: (i ^ 1, j ^ 2))
LAST_DIAGONAL = moves_of((3,), lambda i, j: (i ^ 1, j ^ 1))


def send(array, moves):
    return lax.ppermute(array, AXES, moves)


def moved(names, moves):
    out = [None] * 16
    for source, target in moves:
        out[target] = names[source]
    return out


def whose_blocks():
    own = [(i, j) for i in range(4) for j in range(4)]
    kind = [i ^ j for i, j in own]
    line = moved(own, LINE)
    across = moved(own, ACROSS)
    line_across = moved(line, ACROSS)
    near = moved([own[d] if kind[d] == 0 else across[d] for d in range(16)], NEAR_DIAGONAL)
    far = moved(across, FAR_DIAGONAL)
    last = moved(line, LAST_DIAGONAL)
    diagonal = [(near, far, near, last)[kind[d]][d] for d in range(16)]
    mine = [own, across, line, line_across, diagonal]
    theirs = [moved(names, CORES) for names in mine]
    order = [own, theirs[0], across, theirs[1], line, theirs[2]]
    order += [line_across, diagonal, theirs[4], theirs[3]]
    for d in range(16):
        assert len({tuple(sorted(names[d])) for names in order}) == 10
    return order


def spots(first, count, me):
    order = whose_blocks()[first : first + count]
    codes = [sum((4 * names[d][0] + names[d][1]) << 4 * k for k, names in enumerate(order)) for d in range(16)]
    code = jnp.int32(codes[0])
    for d in range(1, 16):
        code = jnp.where(me == d, codes[d], code)
    places = [jnp.bitwise_and(jnp.right_shift(code, 4 * k), 15) for k in range(count)]
    return [(jnp.right_shift(p, 2), jnp.bitwise_and(p, 3)) for p in places]


def block_at(edge, k):
    return pl.ds(pl.multiple_of(k * edge, 128), edge)


def place(first, blocks, full, sems):
    edge = blocks[0].shape[0]
    me = number(lax.axis_index("wide"), lax.axis_index("narrow"))
    copies = []
    for k, (a, b) in enumerate(spots(first, len(blocks), me)):
        spot, image = (block_at(edge, a), block_at(edge, b)), (block_at(edge, b), block_at(edge, a))
        copy = pltpu.make_async_copy(blocks[k], full.at[spot], sems.at[k])
        copies.append((copy, a != b, spot, image))
    for copy, *_ in copies:
        copy.start()
    return copies


def mirror(copies, full):
    for copy, off_diagonal, spot, image in copies:
        copy.wait()

        @pl.when(off_diagonal)
        def _():
            full[image] = full[spot].T


def early_kernel(*refs):
    blocks, full, sems = refs[:-2], *refs[-2:]
    mirror(place(0, blocks, full, sems), full)


def square_columns(first, count, full, rows, square, low):
    n, edge = rows.shape[0], square.shape[0]
    panel = full[block_at(edge, lax.axis_index("wide"))]
    for t in range(count):
        cols = pl.ds(pl.multiple_of(first + 256 * t, 128), 256)
        s = jnp.dot(panel, full[:, cols], preferred_element_type=F32)
        s = masked(s, rows[:, cols])
        square[:, cols] = s
        low[:, cols] = s.astype(BF16)


def masked(x, rows):
    n = rows.shape[0]
    tall = x.reshape(n, x.shape[0] // n, x.shape[1]) * rows[:, None, :]
    return tall.reshape(x.shape)


def middle_kernel(full_in, *refs):
    blocks, patterns, (full, rows, square, low, small, sems) = refs[:-10], refs[-10:-6], refs[-6:]
    edge, order = square.shape
    n = small.shape[1]
    step = edge // n
    count = len(blocks)
    loads = [pltpu.make_async_copy(p, small.at[k], sems.at[count + k]) for k, p in enumerate(patterns)]
    for load in loads:
        load.start()
    copies = place(6, blocks, full, sems)
    i, j = lax.axis_index("wide"), lax.axis_index("narrow")
    r = lax.broadcasted_iota(jnp.int32, (n, edge), 0)
    c = lax.broadcasted_iota(jnp.int32, (n, edge), 1)
    widen = jnp.where(r == c // step, 1.0, 0.0).astype(BF16)
    for k, load in enumerate(loads):
        load.wait()
        wide = jnp.dot(small[k].astype(BF16), widen, preferred_element_type=F32)
        rows[:, block_at(edge, jnp.bitwise_xor(j, k))] = wide
    mirror(copies, full)

    @pl.when(jnp.right_shift(i, 1) == jnp.right_shift(j, 1))
    def _():
        square_columns(jnp.right_shift(i, 1) * (order // 2), order // 512, full, rows, square, low)


def purify_kernel(full_in, rows, square_in, low_in, *refs):
    blocks, (out, full, square, low, sems) = refs[:-5], refs[-5:]
    edge, order = square.shape
    mirror(place(10 - len(blocks), blocks, full, sems), full)
    i, j = lax.axis_index("wide"), lax.axis_index("narrow")
    half = jnp.right_shift(i, 1)

    @pl.when(half == jnp.right_shift(j, 1))
    def _():
        square_columns((1 - half) * (order // 2), order // 512, full, rows, square, low)

    @pl.when(half != jnp.right_shift(j, 1))
    def _():
        square_columns(0, order // 256, full, rows, square, low)

    mine = block_at(edge, j)
    cube = jnp.dot(low[...], full[:, mine], preferred_element_type=F32)
    cube = masked(cube, rows[:, mine])
    out[...] = (3.0 * square[:, mine] - 2.0 * cube).astype(BF16)


VMEM = pl.BlockSpec(memory_space=pltpu.VMEM)
HBM = pl.BlockSpec(memory_space=pl.ANY)
PARAMS = pltpu.CompilerParams(vmem_limit_bytes=24 << 20)


def in_vmem(array):
    return pltpu.with_memory_space_constraint(array, pltpu.VMEM)


def early(blocks):
    order = 4 * blocks[0].shape[0]
    return pl.pallas_call(
        early_kernel,
        out_shape=pltpu.VMEM((order, order), BF16),
        in_specs=[HBM] * len(blocks),
        out_specs=VMEM,
        scratch_shapes=[pltpu.SemaphoreType.DMA((len(blocks),))],
        compiler_params=PARAMS,
        name="early",
    )(*blocks)


def middle(full, blocks, patterns):
    order = full.shape[0]
    edge = order // 4
    n = patterns[0].shape[0]
    return pl.pallas_call(
        middle_kernel,
        out_shape=(
            pltpu.VMEM((order, order), BF16),
            pltpu.VMEM((n, order), F32),
            pltpu.VMEM((edge, order), F32),
            pltpu.VMEM((edge, order), BF16),
        ),
        in_specs=[VMEM] + [HBM] * (len(blocks) + 4),
        out_specs=(VMEM,) * 4,
        input_output_aliases={0: 0},
        scratch_shapes=[
            pltpu.VMEM((4, n, n), jnp.int32),
            pltpu.SemaphoreType.DMA((len(blocks) + 4,)),
        ],
        compiler_params=PARAMS,
        name="middle",
    )(in_vmem(full), *blocks, *patterns)


def purify(full, rows, square, low, blocks):
    edge, order = square.shape
    return pl.pallas_call(
        purify_kernel,
        out_shape=(
            jax.ShapeDtypeStruct((edge, edge), BF16),
            pltpu.VMEM((order, order), BF16),
            pltpu.VMEM((edge, order), F32),
            pltpu.VMEM((edge, order), BF16),
        ),
        in_specs=[VMEM] * 4 + [HBM] * len(blocks),
        out_specs=(VMEM,) * 4,
        input_output_aliases={0: 1, 2: 2, 3: 3},
        scratch_shapes=[pltpu.SemaphoreType.DMA((len(blocks),))],
        compiler_params=PARAMS,
        name="purify",
    )(*map(in_vmem, (full, rows, square, low)), *blocks)[0]


def block_body(own, pattern):
    i, j = lax.axis_index("wide"), lax.axis_index("narrow")
    kind = jnp.bitwise_xor(i, j)
    hold = lax.optimization_barrier
    line, across = send(own, LINE), send(own, ACROSS)
    near = send(jnp.where(kind == 0, own, across), NEAR_DIAGONAL)
    far = send(across, FAR_DIAGONAL)
    own_c, across_c = send(own, CORES), send(across, CORES)
    own_c, across_c, line = hold((own_c, across_c, line))
    line_across, last = send(line, ACROSS), send(line, LAST_DIAGONAL)
    line_c = send(line, CORES)
    pattern, line = hold((pattern, line))
    got = {k: lax.ppermute(pattern, "narrow", [(c, c ^ k) for c in range(4)]) for k in (1, 2, 3)}
    patterns = [pattern, got[1], got[2], got[3]]
    full = early((own, own_c, across, across_c, line, line_c))
    patterns, full = hold((patterns, full))
    line_across, full = hold((line_across, full))
    line_across_c = send(line_across, CORES)
    diagonal = jnp.where(kind == 3, last, jnp.where(kind == 1, far, near))
    diagonal_c = send(diagonal, CORES)
    full, rows, square, low = middle(full, (line_across, diagonal, diagonal_c), patterns)
    return purify(full, rows, square, low, (line_across_c,))


def solution(mesh):
    four = mesh.shape["wide"] == 4 and mesh.shape["narrow"] == 4

    def body(density, pattern):
        rows, cols = density.shape
        fits = rows == cols and rows % 128 == 0 and rows <= 512
        fits = fits and pattern.shape[0] == pattern.shape[1] <= 16
        return (block_body if four and fits else panel_body)(density, pattern)

    return jax.shard_map(
        body,
        mesh=mesh,
        in_specs=(P(("groups", "wide"), "narrow"), P(("groups", "wide"), "narrow")),
        out_specs=P(("groups", "wide"), "narrow"),
        check_vma=False,
    )
```

```python
import jax
import jax.numpy as jnp
from jax import lax
from jax.experimental import pallas as pl
from jax.experimental.pallas import tpu as pltpu
from jax.sharding import PartitionSpec as P

AXES = ("wide", "narrow")
F32, BF16 = jnp.float32, jnp.bfloat16


def expand(pattern, row_count, col_count):
    block_rows, block_cols = pattern.shape
    block_edge = row_count // block_rows
    spread_out = jnp.broadcast_to(
        pattern[:, None, :, None], (block_rows, block_edge, block_cols, block_edge)
    )
    return spread_out.reshape(row_count, col_count).astype(jnp.float32)


def panel_body(density, pattern):
    row_count, col_count = density.shape
    tile_mask = expand(pattern, row_count, col_count)
    row_panel = lax.all_gather(density, "narrow", axis=1, tiled=True)
    col_panel = lax.all_gather(density, "wide", axis=0, tiled=True)
    square = jnp.dot(row_panel, col_panel, preferred_element_type=F32) * tile_mask
    square_low = square.astype(BF16)
    square_panel = lax.all_gather(square_low, "narrow", axis=1, tiled=True)
    cube_sum = jnp.dot(square_panel, col_panel, preferred_element_type=F32) * tile_mask
    return (3.0 * square - 2.0 * cube_sum).astype(BF16)


def number(i, j):
    return 4 * i + j


def turned(moves):
    other = [((3 - a, 3 - b), (3 - c, 3 - d)) for (a, b), (c, d) in moves]
    return [(number(*s), number(*t)) for s, t in moves + other]


def moves_of(kinds, target):
    grid = [(i, j) for i in range(4) for j in range(4) if i ^ j in kinds]
    return [(number(i, j), number(*target(i, j))) for i, j in grid]


LINE = turned(
    [
        ((2, 0), (3, 3)),
        ((2, 1), (2, 3)),
        ((3, 0), (2, 2)),
        ((3, 1), (3, 2)),
        ((2, 2), (2, 1)),
        ((3, 2), (3, 1)),
        ((2, 3), (2, 0)),
        ((3, 3), (3, 0)),
    ]
)
ACROSS = moves_of((0, 1, 2, 3), lambda i, j: (i ^ 2, j))
CORES = moves_of((0, 1, 2, 3), lambda i, j: (i ^ 1, j))
NEAR_DIAGONAL = moves_of((0, 2), lambda i, j: (i ^ 1, j ^ 1))
FAR_DIAGONAL = moves_of((2,), lambda i, j: (i ^ 1, j ^ 2))
LAST_DIAGONAL = moves_of((3,), lambda i, j: (i ^ 1, j ^ 1))


def send(array, moves):
    return lax.ppermute(array, AXES, moves)


def moved(names, moves):
    out = [None] * 16
    for source, target in moves:
        out[target] = names[source]
    return out


def whose_blocks():
    own = [(i, j) for i in range(4) for j in range(4)]
    kind = [i ^ j for i, j in own]
    line = moved(own, LINE)
    across = moved(own, ACROSS)
    line_across = moved(line, ACROSS)
    near = moved([own[d] if kind[d] == 0 else across[d] for d in range(16)], NEAR_DIAGONAL)
    far = moved(across, FAR_DIAGONAL)
    last = moved(line, LAST_DIAGONAL)
    diagonal = [(near, far, near, last)[kind[d]][d] for d in range(16)]
    mine = [own, across, line, line_across, diagonal]
    theirs = [moved(names, CORES) for names in mine]
    order = [own, theirs[0], across, theirs[1], line, theirs[2]]
    order += [line_across, diagonal, theirs[4], theirs[3]]
    for d in range(16):
        assert len({tuple(sorted(names[d])) for names in order}) == 10
    return order


def spots(first, count, me):
    order = whose_blocks()[first : first + count]
    codes = [sum((4 * names[d][0] + names[d][1]) << 4 * k for k, names in enumerate(order)) for d in range(16)]
    code = jnp.int32(codes[0])
    for d in range(1, 16):
        code = jnp.where(me == d, codes[d], code)
    places = [jnp.bitwise_and(jnp.right_shift(code, 4 * k), 15) for k in range(count)]
    return [(jnp.right_shift(p, 2), jnp.bitwise_and(p, 3)) for p in places]


def block_at(edge, k):
    return pl.ds(pl.multiple_of(k * edge, 128), edge)


def place(first, blocks, full, sems):
    edge = blocks[0].shape[0]
    me = number(lax.axis_index("wide"), lax.axis_index("narrow"))
    copies = []
    for k, (a, b) in enumerate(spots(first, len(blocks), me)):
        spot, image = (block_at(edge, a), block_at(edge, b)), (block_at(edge, b), block_at(edge, a))
        copy = pltpu.make_async_copy(blocks[k], full.at[spot], sems.at[k])
        copies.append((copy, a != b, spot, image))
    for copy, *_ in copies:
        copy.start()
    return copies


def mirror(copies, full):
    for copy, off_diagonal, spot, image in copies:
        copy.wait()

        @pl.when(off_diagonal)
        def _():
            full[image] = full[spot].T


def early_kernel(*refs):
    blocks, full, sems = refs[:-2], *refs[-2:]
    mirror(place(0, blocks, full, sems), full)


def square_columns(first, count, full, rows, square, low):
    n, edge = rows.shape[0], square.shape[0]
    panel = full[block_at(edge, lax.axis_index("wide"))]
    for t in range(count):
        cols = pl.ds(pl.multiple_of(first + 256 * t, 128), 256)
        s = jnp.dot(panel, full[:, cols], preferred_element_type=F32)
        s = masked(s, rows[:, cols])
        square[:, cols] = s
        low[:, cols] = s.astype(BF16)


def masked(x, rows):
    n = rows.shape[0]
    tall = x.reshape(n, x.shape[0] // n, x.shape[1]) * rows[:, None, :]
    return tall.reshape(x.shape)


def middle_kernel(full_in, *refs):
    blocks, patterns, (full, rows, square, low, small, sems) = refs[:-10], refs[-10:-6], refs[-6:]
    edge, order = square.shape
    n = small.shape[1]
    step = edge // n
    count = len(blocks)
    loads = [pltpu.make_async_copy(p, small.at[k], sems.at[count + k]) for k, p in enumerate(patterns)]
    for load in loads:
        load.start()
    copies = place(6, blocks, full, sems)
    i, j = lax.axis_index("wide"), lax.axis_index("narrow")
    r = lax.broadcasted_iota(jnp.int32, (n, edge), 0)
    c = lax.broadcasted_iota(jnp.int32, (n, edge), 1)
    widen = jnp.where(r == c // step, 1.0, 0.0).astype(BF16)
    for k, load in enumerate(loads):
        load.wait()
        wide = jnp.dot(small[k].astype(BF16), widen, preferred_element_type=F32)
        rows[:, block_at(edge, jnp.bitwise_xor(j, k))] = wide
    mirror(copies, full)

    @pl.when(jnp.right_shift(i, 1) == jnp.right_shift(j, 1))
    def _():
        square_columns(jnp.right_shift(i, 1) * (order // 2), order // 512, full, rows, square, low)


def purify_kernel(full_in, rows, square_in, low_in, *refs):
    blocks, (out, full, square, low, result, sems, done) = refs[:-7], refs[-7:]
    edge, order = square.shape
    mirror(place(10 - len(blocks), blocks, full, sems), full)
    i, j = lax.axis_index("wide"), lax.axis_index("narrow")
    half = jnp.right_shift(i, 1)

    @pl.when(half == jnp.right_shift(j, 1))
    def _():
        square_columns((1 - half) * (order // 2), order // 512, full, rows, square, low)

    @pl.when(half != jnp.right_shift(j, 1))
    def _():
        square_columns(0, order // 256, full, rows, square, low)

    mine = block_at(edge, j)
    n = rows.shape[0]
    writes = []
    for part in range(2):
        some = slice(part * edge // 2, (part + 1) * edge // 2)
        cube = jnp.dot(low[some], full[:, mine], preferred_element_type=F32)
        cube = masked(cube, rows[part * n // 2 : (part + 1) * n // 2, mine])
        result[some] = (3.0 * square[some, mine] - 2.0 * cube).astype(BF16)
        writes.append(pltpu.make_async_copy(result.at[some], out.at[some], done.at[part]))
        writes[-1].start()
    for write in writes:
        write.wait()


VMEM = pl.BlockSpec(memory_space=pltpu.VMEM)
HBM = pl.BlockSpec(memory_space=pl.ANY)
PARAMS = pltpu.CompilerParams(vmem_limit_bytes=24 << 20)


def in_vmem(array):
    return pltpu.with_memory_space_constraint(array, pltpu.VMEM)


def early(blocks):
    order = 4 * blocks[0].shape[0]
    return pl.pallas_call(
        early_kernel,
        out_shape=pltpu.VMEM((order, order), BF16),
        in_specs=[HBM] * len(blocks),
        out_specs=VMEM,
        scratch_shapes=[pltpu.SemaphoreType.DMA((len(blocks),))],
        compiler_params=PARAMS,
        name="early",
    )(*blocks)


def middle(full, blocks, patterns):
    order = full.shape[0]
    edge = order // 4
    n = patterns[0].shape[0]
    return pl.pallas_call(
        middle_kernel,
        out_shape=(
            pltpu.VMEM((order, order), BF16),
            pltpu.VMEM((n, order), F32),
            pltpu.VMEM((edge, order), F32),
            pltpu.VMEM((edge, order), BF16),
        ),
        in_specs=[VMEM] + [HBM] * (len(blocks) + 4),
        out_specs=(VMEM,) * 4,
        input_output_aliases={0: 0},
        scratch_shapes=[
            pltpu.VMEM((4, n, n), jnp.int32),
            pltpu.SemaphoreType.DMA((len(blocks) + 4,)),
        ],
        compiler_params=PARAMS,
        name="middle",
    )(in_vmem(full), *blocks, *patterns)


def purify(full, rows, square, low, blocks):
    edge, order = square.shape
    return pl.pallas_call(
        purify_kernel,
        out_shape=(
            jax.ShapeDtypeStruct((edge, edge), BF16),
            pltpu.VMEM((order, order), BF16),
            pltpu.VMEM((edge, order), F32),
            pltpu.VMEM((edge, order), BF16),
        ),
        in_specs=[VMEM] * 4 + [HBM] * len(blocks),
        out_specs=(HBM,) + (VMEM,) * 3,
        input_output_aliases={0: 1, 2: 2, 3: 3},
        scratch_shapes=[
            pltpu.VMEM((edge, edge), BF16),
            pltpu.SemaphoreType.DMA((len(blocks),)),
            pltpu.SemaphoreType.DMA((2,)),
        ],
        compiler_params=PARAMS,
        name="purify",
    )(*map(in_vmem, (full, rows, square, low)), *blocks)[0]


def block_body(own, pattern):
    i, j = lax.axis_index("wide"), lax.axis_index("narrow")
    kind = jnp.bitwise_xor(i, j)
    hold = lax.optimization_barrier
    line, across = send(own, LINE), send(own, ACROSS)
    near = send(jnp.where(kind == 0, own, across), NEAR_DIAGONAL)
    far = send(across, FAR_DIAGONAL)
    own_c, across_c = send(own, CORES), send(across, CORES)
    own_c, across_c, line = hold((own_c, across_c, line))
    line_across, last = send(line, ACROSS), send(line, LAST_DIAGONAL)
    line_c = send(line, CORES)
    pattern, line = hold((pattern, line))
    got = {k: lax.ppermute(pattern, "narrow", [(c, c ^ k) for c in range(4)]) for k in (1, 2, 3)}
    patterns = [pattern, got[1], got[2], got[3]]
    full = early((own, own_c, across, across_c, line, line_c))
    patterns, full = hold((patterns, full))
    line_across, full = hold((line_across, full))
    line_across_c = send(line_across, CORES)
    diagonal = jnp.where(kind == 3, last, jnp.where(kind == 1, far, near))
    diagonal_c = send(diagonal, CORES)
    full, rows, square, low = middle(full, (line_across, diagonal, diagonal_c), patterns)
    return purify(full, rows, square, low, (line_across_c,))


def solution(mesh):
    four = mesh.shape["wide"] == 4 and mesh.shape["narrow"] == 4

    def body(density, pattern):
        rows, cols = density.shape
        fits = rows == cols and rows % 128 == 0 and rows <= 512
        fits = fits and pattern.shape[0] == pattern.shape[1] <= 16
        fits = fits and pattern.shape[0] % 2 == 0
        return (block_body if four and fits else panel_body)(density, pattern)

    return jax.shard_map(
        body,
        mesh=mesh,
        in_specs=(P(("groups", "wide"), "narrow"), P(("groups", "wide"), "narrow")),
        out_specs=P(("groups", "wide"), "narrow"),
        check_vma=False,
    )
```

```python
import jax
import jax.numpy as jnp
from jax import lax
from jax.experimental import pallas as pl
from jax.experimental.pallas import tpu as pltpu
from jax.sharding import PartitionSpec as P

AXES = ("wide", "narrow")
F32, BF16 = jnp.float32, jnp.bfloat16


def expand(pattern, row_count, col_count):
    block_rows, block_cols = pattern.shape
    block_edge = row_count // block_rows
    spread_out = jnp.broadcast_to(
        pattern[:, None, :, None], (block_rows, block_edge, block_cols, block_edge)
    )
    return spread_out.reshape(row_count, col_count).astype(jnp.float32)


def panel_body(density, pattern):
    row_count, col_count = density.shape
    tile_mask = expand(pattern, row_count, col_count)
    row_panel = lax.all_gather(density, "narrow", axis=1, tiled=True)
    col_panel = lax.all_gather(density, "wide", axis=0, tiled=True)
    square = jnp.dot(row_panel, col_panel, preferred_element_type=F32) * tile_mask
    square_low = square.astype(BF16)
    square_panel = lax.all_gather(square_low, "narrow", axis=1, tiled=True)
    cube_sum = jnp.dot(square_panel, col_panel, preferred_element_type=F32) * tile_mask
    return (3.0 * square - 2.0 * cube_sum).astype(BF16)


def number(i, j):
    return 4 * i + j


def turned(moves):
    other = [((3 - a, 3 - b), (3 - c, 3 - d)) for (a, b), (c, d) in moves]
    return [(number(*s), number(*t)) for s, t in moves + other]


def moves_of(kinds, target):
    grid = [(i, j) for i in range(4) for j in range(4) if i ^ j in kinds]
    return [(number(i, j), number(*target(i, j))) for i, j in grid]


LINE = turned(
    [
        ((2, 0), (3, 3)),
        ((2, 1), (2, 3)),
        ((3, 0), (2, 2)),
        ((3, 1), (3, 2)),
        ((2, 2), (2, 1)),
        ((3, 2), (3, 1)),
        ((2, 3), (2, 0)),
        ((3, 3), (3, 0)),
    ]
)
ACROSS = moves_of((0, 1, 2, 3), lambda i, j: (i ^ 2, j))
CORES = moves_of((0, 1, 2, 3), lambda i, j: (i ^ 1, j))
NEAR_DIAGONAL = moves_of((0, 2), lambda i, j: (i ^ 1, j ^ 1))
FAR_DIAGONAL = moves_of((2,), lambda i, j: (i ^ 1, j ^ 2))
LAST_DIAGONAL = moves_of((3,), lambda i, j: (i ^ 1, j ^ 1))


def send(array, moves):
    return lax.ppermute(array, AXES, moves)


def moved(names, moves):
    out = [None] * 16
    for source, target in moves:
        out[target] = names[source]
    return out


def whose_blocks():
    own = [(i, j) for i in range(4) for j in range(4)]
    kind = [i ^ j for i, j in own]
    line = moved(own, LINE)
    across = moved(own, ACROSS)
    line_across = moved(line, ACROSS)
    near = moved([own[d] if kind[d] == 0 else across[d] for d in range(16)], NEAR_DIAGONAL)
    far = moved(across, FAR_DIAGONAL)
    last = moved(line, LAST_DIAGONAL)
    diagonal = [(near, far, near, last)[kind[d]][d] for d in range(16)]
    mine = [own, across, line, line_across, diagonal]
    theirs = [moved(names, CORES) for names in mine]
    order = [own, theirs[0], across, theirs[1], line, theirs[2]]
    order += [line_across, diagonal, theirs[4], theirs[3]]
    for d in range(16):
        assert len({tuple(sorted(names[d])) for names in order}) == 10
    return order


def spots(first, count, me):
    order = whose_blocks()[first : first + count]
    codes = [sum((4 * names[d][0] + names[d][1]) << 4 * k for k, names in enumerate(order)) for d in range(16)]
    code = jnp.int32(codes[0])
    for d in range(1, 16):
        code = jnp.where(me == d, codes[d], code)
    places = [jnp.bitwise_and(jnp.right_shift(code, 4 * k), 15) for k in range(count)]
    return [(jnp.right_shift(p, 2), jnp.bitwise_and(p, 3)) for p in places]


def block_at(edge, k):
    return pl.ds(pl.multiple_of(k * edge, 128), edge)


def place(first, blocks, full, sems):
    edge = blocks[0].shape[0]
    me = number(lax.axis_index("wide"), lax.axis_index("narrow"))
    copies = []
    for k, (a, b) in enumerate(spots(first, len(blocks), me)):
        spot, image = (block_at(edge, a), block_at(edge, b)), (block_at(edge, b), block_at(edge, a))
        copy = pltpu.make_async_copy(blocks[k], full.at[spot], sems.at[k])
        copies.append((copy, a != b, spot, image))
    for copy, *_ in copies:
        copy.start()
    return copies


def mirror(copies, full):
    for copy, off_diagonal, spot, image in copies:
        copy.wait()

        @pl.when(off_diagonal)
        def _():
            full[image] = full[spot].T


def early_kernel(*refs):
    blocks, full, sems = refs[:-2], *refs[-2:]
    mirror(place(0, blocks, full, sems), full)


def square_columns(first, count, full, rows, square, low):
    n, edge = rows.shape[0], square.shape[0]
    panel = full[block_at(edge, lax.axis_index("wide"))]
    for t in range(count):
        cols = pl.ds(pl.multiple_of(first + 256 * t, 128), 256)
        s = jnp.dot(panel, full[:, cols], preferred_element_type=F32)
        square[:, cols] = s
        low[:, cols] = masked(s, rows[:, cols]).astype(BF16)


def masked(x, rows):
    n = rows.shape[0]
    tall = x.reshape(n, x.shape[0] // n, x.shape[1]) * rows[:, None, :]
    return tall.reshape(x.shape)


def middle_kernel(full_in, *refs):
    blocks, patterns, (full, rows, square, low, small, sems) = refs[:-10], refs[-10:-6], refs[-6:]
    edge, order = square.shape
    n = small.shape[1]
    step = edge // n
    count = len(blocks)
    loads = [pltpu.make_async_copy(p, small.at[k], sems.at[count + k]) for k, p in enumerate(patterns)]
    for load in loads:
        load.start()
    copies = place(6, blocks, full, sems)
    i, j = lax.axis_index("wide"), lax.axis_index("narrow")
    r = lax.broadcasted_iota(jnp.int32, (n, edge), 0)
    c = lax.broadcasted_iota(jnp.int32, (n, edge), 1)
    widen = jnp.where(r == c // step, 1.0, 0.0).astype(BF16)
    for k, load in enumerate(loads):
        load.wait()
        wide = jnp.dot(small[k].astype(BF16), widen, preferred_element_type=F32)
        rows[:, block_at(edge, jnp.bitwise_xor(j, k))] = wide
    mirror(copies, full)

    @pl.when(jnp.right_shift(i, 1) == jnp.right_shift(j, 1))
    def _():
        square_columns(jnp.right_shift(i, 1) * (order // 2), order // 512, full, rows, square, low)


def purify_kernel(full_in, rows, square_in, low_in, *refs):
    blocks, (out, full, square, low, sems) = refs[:-5], refs[-5:]
    edge, order = square.shape
    mirror(place(10 - len(blocks), blocks, full, sems), full)
    i, j = lax.axis_index("wide"), lax.axis_index("narrow")
    half = jnp.right_shift(i, 1)

    @pl.when(half == jnp.right_shift(j, 1))
    def _():
        square_columns((1 - half) * (order // 2), order // 512, full, rows, square, low)

    @pl.when(half != jnp.right_shift(j, 1))
    def _():
        square_columns(0, order // 256, full, rows, square, low)

    mine = block_at(edge, j)
    cube = jnp.dot(low[...], full[:, mine], preferred_element_type=F32)
    out[...] = masked(3.0 * square[:, mine] - 2.0 * cube, rows[:, mine]).astype(BF16)


VMEM = pl.BlockSpec(memory_space=pltpu.VMEM)
HBM = pl.BlockSpec(memory_space=pl.ANY)
PARAMS = pltpu.CompilerParams(vmem_limit_bytes=24 << 20)


def in_vmem(array):
    return pltpu.with_memory_space_constraint(array, pltpu.VMEM)


def early(blocks):
    order = 4 * blocks[0].shape[0]
    return pl.pallas_call(
        early_kernel,
        out_shape=pltpu.VMEM((order, order), BF16),
        in_specs=[HBM] * len(blocks),
        out_specs=VMEM,
        scratch_shapes=[pltpu.SemaphoreType.DMA((len(blocks),))],
        compiler_params=PARAMS,
        name="early",
    )(*blocks)


def middle(full, blocks, patterns):
    order = full.shape[0]
    edge = order // 4
    n = patterns[0].shape[0]
    return pl.pallas_call(
        middle_kernel,
        out_shape=(
            pltpu.VMEM((order, order), BF16),
            pltpu.VMEM((n, order), F32),
            pltpu.VMEM((edge, order), F32),
            pltpu.VMEM((edge, order), BF16),
        ),
        in_specs=[VMEM] + [HBM] * (len(blocks) + 4),
        out_specs=(VMEM,) * 4,
        input_output_aliases={0: 0},
        scratch_shapes=[
            pltpu.VMEM((4, n, n), jnp.int32),
            pltpu.SemaphoreType.DMA((len(blocks) + 4,)),
        ],
        compiler_params=PARAMS,
        name="middle",
    )(in_vmem(full), *blocks, *patterns)


def purify(full, rows, square, low, blocks):
    edge, order = square.shape
    return pl.pallas_call(
        purify_kernel,
        out_shape=(
            jax.ShapeDtypeStruct((edge, edge), BF16),
            pltpu.VMEM((order, order), BF16),
            pltpu.VMEM((edge, order), F32),
            pltpu.VMEM((edge, order), BF16),
        ),
        in_specs=[VMEM] * 4 + [HBM] * len(blocks),
        out_specs=(VMEM,) * 4,
        input_output_aliases={0: 1, 2: 2, 3: 3},
        scratch_shapes=[pltpu.SemaphoreType.DMA((len(blocks),))],
        compiler_params=PARAMS,
        name="purify",
    )(*map(in_vmem, (full, rows, square, low)), *blocks)[0]


def block_body(own, pattern):
    i, j = lax.axis_index("wide"), lax.axis_index("narrow")
    kind = jnp.bitwise_xor(i, j)
    hold = lax.optimization_barrier
    line, across = send(own, LINE), send(own, ACROSS)
    near = send(jnp.where(kind == 0, own, across), NEAR_DIAGONAL)
    far = send(across, FAR_DIAGONAL)
    own_c, across_c = send(own, CORES), send(across, CORES)
    own_c, across_c, line = hold((own_c, across_c, line))
    line_across, last = send(line, ACROSS), send(line, LAST_DIAGONAL)
    line_c = send(line, CORES)
    pattern, line = hold((pattern, line))
    got = {k: lax.ppermute(pattern, "narrow", [(c, c ^ k) for c in range(4)]) for k in (1, 2, 3)}
    patterns = [pattern, got[1], got[2], got[3]]
    full = early((own, own_c, across, across_c, line, line_c))
    patterns, full = hold((patterns, full))
    line_across, full = hold((line_across, full))
    line_across_c = send(line_across, CORES)
    diagonal = jnp.where(kind == 3, last, jnp.where(kind == 1, far, near))
    diagonal_c = send(diagonal, CORES)
    full, rows, square, low = middle(full, (line_across, diagonal, diagonal_c), patterns)
    return purify(full, rows, square, low, (line_across_c,))


def solution(mesh):
    four = mesh.shape["wide"] == 4 and mesh.shape["narrow"] == 4

    def body(density, pattern):
        rows, cols = density.shape
        fits = rows == cols and rows % 128 == 0 and rows <= 512
        fits = fits and pattern.shape[0] == pattern.shape[1] <= 16
        return (block_body if four and fits else panel_body)(density, pattern)

    return jax.shard_map(
        body,
        mesh=mesh,
        in_specs=(P(("groups", "wide"), "narrow"), P(("groups", "wide"), "narrow")),
        out_specs=P(("groups", "wide"), "narrow"),
        check_vma=False,
    )
```

```python
import jax
import jax.numpy as jnp
from jax import lax
from jax.experimental import pallas as pl
from jax.experimental.pallas import tpu as pltpu
from jax.sharding import PartitionSpec as P

AXES = ("wide", "narrow")
F32, BF16 = jnp.float32, jnp.bfloat16


def expand(pattern, row_count, col_count):
    block_rows, block_cols = pattern.shape
    block_edge = row_count // block_rows
    spread_out = jnp.broadcast_to(
        pattern[:, None, :, None], (block_rows, block_edge, block_cols, block_edge)
    )
    return spread_out.reshape(row_count, col_count).astype(jnp.float32)


def panel_body(density, pattern):
    row_count, col_count = density.shape
    tile_mask = expand(pattern, row_count, col_count)
    row_panel = lax.all_gather(density, "narrow", axis=1, tiled=True)
    col_panel = lax.all_gather(density, "wide", axis=0, tiled=True)
    square = jnp.dot(row_panel, col_panel, preferred_element_type=F32) * tile_mask
    square_low = square.astype(BF16)
    square_panel = lax.all_gather(square_low, "narrow", axis=1, tiled=True)
    cube_sum = jnp.dot(square_panel, col_panel, preferred_element_type=F32) * tile_mask
    return (3.0 * square - 2.0 * cube_sum).astype(BF16)


def number(i, j):
    return 4 * i + j


def turned(moves):
    other = [((3 - a, 3 - b), (3 - c, 3 - d)) for (a, b), (c, d) in moves]
    return [(number(*s), number(*t)) for s, t in moves + other]


def moves_of(kinds, target):
    grid = [(i, j) for i in range(4) for j in range(4) if i ^ j in kinds]
    return [(number(i, j), number(*target(i, j))) for i, j in grid]


LINE = turned(
    [
        ((2, 0), (3, 3)),
        ((2, 1), (2, 3)),
        ((3, 0), (2, 2)),
        ((3, 1), (3, 2)),
        ((2, 2), (2, 1)),
        ((3, 2), (3, 1)),
        ((2, 3), (2, 0)),
        ((3, 3), (3, 0)),
    ]
)
ACROSS = moves_of((0, 1, 2, 3), lambda i, j: (i ^ 2, j))
CORES = moves_of((0, 1, 2, 3), lambda i, j: (i ^ 1, j))
NEAR_DIAGONAL = moves_of((0, 2), lambda i, j: (i ^ 1, j ^ 1))
FAR_DIAGONAL = moves_of((2,), lambda i, j: (i ^ 1, j ^ 2))
LAST_DIAGONAL = moves_of((3,), lambda i, j: (i ^ 1, j ^ 1))


def send(array, moves):
    return lax.ppermute(array, AXES, moves)


def moved(names, moves):
    out = [None] * 16
    for source, target in moves:
        out[target] = names[source]
    return out


def whose_blocks():
    own = [(i, j) for i in range(4) for j in range(4)]
    kind = [i ^ j for i, j in own]
    line = moved(own, LINE)
    across = moved(own, ACROSS)
    line_across = moved(line, ACROSS)
    near = moved([own[d] if kind[d] == 0 else across[d] for d in range(16)], NEAR_DIAGONAL)
    far = moved(across, FAR_DIAGONAL)
    last = moved(line, LAST_DIAGONAL)
    diagonal = [(near, far, near, last)[kind[d]][d] for d in range(16)]
    mine = [own, across, line, line_across, diagonal]
    theirs = [moved(names, CORES) for names in mine]
    order = [own, theirs[0], across, theirs[1], line, theirs[2]]
    order += [line_across, diagonal, theirs[4], theirs[3]]
    for d in range(16):
        assert len({tuple(sorted(names[d])) for names in order}) == 10
    return order


def spots(first, count, me):
    order = whose_blocks()[first : first + count]
    codes = [sum((4 * names[d][0] + names[d][1]) << 4 * k for k, names in enumerate(order)) for d in range(16)]
    code = jnp.int32(codes[0])
    for d in range(1, 16):
        code = jnp.where(me == d, codes[d], code)
    places = [jnp.bitwise_and(jnp.right_shift(code, 4 * k), 15) for k in range(count)]
    return [(jnp.right_shift(p, 2), jnp.bitwise_and(p, 3)) for p in places]


def block_at(edge, k):
    return pl.ds(pl.multiple_of(k * edge, 128), edge)


def place(first, blocks, full, sems):
    edge = blocks[0].shape[0]
    me = number(lax.axis_index("wide"), lax.axis_index("narrow"))
    copies = []
    for k, (a, b) in enumerate(spots(first, len(blocks), me)):
        spot, image = (block_at(edge, a), block_at(edge, b)), (block_at(edge, b), block_at(edge, a))
        copy = pltpu.make_async_copy(blocks[k], full.at[spot], sems.at[k])
        copies.append((copy, a != b, spot, image))
    for copy, *_ in copies:
        copy.start()
    return copies


def mirror(copies, full):
    for copy, off_diagonal, spot, image in copies:
        copy.wait()

        @pl.when(off_diagonal)
        def _():
            full[image] = full[spot].T


def early_kernel(*refs):
    blocks, full, sems = refs[:-2], *refs[-2:]
    mirror(place(0, blocks, full, sems), full)


def square_columns(first, count, full, rows, square, low):
    n, edge = rows.shape[0], square.shape[0]
    panel = full[block_at(edge, lax.axis_index("wide"))]
    for t in range(count):
        cols = pl.ds(pl.multiple_of(first + 256 * t, 128), 256)
        s = jnp.dot(panel, full[:, cols], preferred_element_type=F32)
        square[:, cols] = s
        low[:, cols] = masked(s, rows[:, cols]).astype(BF16)


def masked(x, rows):
    n = rows.shape[0]
    tall = x.reshape(n, x.shape[0] // n, x.shape[1]) * rows[:, None, :]
    return tall.reshape(x.shape)


def middle_kernel(full_in, *refs):
    blocks, patterns, (full, rows, square, low, small, sems) = refs[:-10], refs[-10:-6], refs[-6:]
    edge, order = square.shape
    n = small.shape[1]
    step = edge // n
    count = len(blocks)
    loads = [pltpu.make_async_copy(p, small.at[k], sems.at[count + k]) for k, p in enumerate(patterns)]
    for load in loads:
        load.start()
    copies = place(6, blocks, full, sems)
    i, j = lax.axis_index("wide"), lax.axis_index("narrow")
    r = lax.broadcasted_iota(jnp.int32, (n, edge), 0)
    c = lax.broadcasted_iota(jnp.int32, (n, edge), 1)
    widen = jnp.where(r == c // step, 1.0, 0.0).astype(BF16)
    for k, load in enumerate(loads):
        load.wait()
        wide = jnp.dot(small[k].astype(BF16), widen, preferred_element_type=F32)
        rows[:, block_at(edge, jnp.bitwise_xor(j, k))] = wide
    mirror(copies, full)

    @pl.when(jnp.right_shift(i, 1) == jnp.right_shift(j, 1))
    def _():
        square_columns(jnp.right_shift(i, 1) * (order // 2), order // 512, full, rows, square, low)


def purify_kernel(full_in, rows, square_in, low_in, *refs):
    blocks, (out, full, square, low, result, sems, done) = refs[:-7], refs[-7:]
    edge, order = square.shape
    mirror(place(10 - len(blocks), blocks, full, sems), full)
    i, j = lax.axis_index("wide"), lax.axis_index("narrow")
    half = jnp.right_shift(i, 1)

    @pl.when(half == jnp.right_shift(j, 1))
    def _():
        square_columns((1 - half) * (order // 2), order // 512, full, rows, square, low)

    @pl.when(half != jnp.right_shift(j, 1))
    def _():
        square_columns(0, order // 256, full, rows, square, low)

    mine = block_at(edge, j)
    n = rows.shape[0]
    writes = []
    for part in range(2):
        some = slice(part * edge // 2, (part + 1) * edge // 2)
        cube = jnp.dot(low[some], full[:, mine], preferred_element_type=F32)
        both = 3.0 * square[some, mine] - 2.0 * cube
        both = masked(both, rows[part * n // 2 : (part + 1) * n // 2, mine])
        result[some] = both.astype(BF16)
        writes.append(pltpu.make_async_copy(result.at[some], out.at[some], done.at[part]))
        writes[-1].start()
    for write in writes:
        write.wait()


VMEM = pl.BlockSpec(memory_space=pltpu.VMEM)
HBM = pl.BlockSpec(memory_space=pl.ANY)
PARAMS = pltpu.CompilerParams(vmem_limit_bytes=24 << 20)


def in_vmem(array):
    return pltpu.with_memory_space_constraint(array, pltpu.VMEM)


def early(blocks):
    order = 4 * blocks[0].shape[0]
    return pl.pallas_call(
        early_kernel,
        out_shape=pltpu.VMEM((order, order), BF16),
        in_specs=[HBM] * len(blocks),
        out_specs=VMEM,
        scratch_shapes=[pltpu.SemaphoreType.DMA((len(blocks),))],
        compiler_params=PARAMS,
        name="early",
    )(*blocks)


def middle(full, blocks, patterns):
    order = full.shape[0]
    edge = order // 4
    n = patterns[0].shape[0]
    return pl.pallas_call(
        middle_kernel,
        out_shape=(
            pltpu.VMEM((order, order), BF16),
            pltpu.VMEM((n, order), F32),
            pltpu.VMEM((edge, order), F32),
            pltpu.VMEM((edge, order), BF16),
        ),
        in_specs=[VMEM] + [HBM] * (len(blocks) + 4),
        out_specs=(VMEM,) * 4,
        input_output_aliases={0: 0},
        scratch_shapes=[
            pltpu.VMEM((4, n, n), jnp.int32),
            pltpu.SemaphoreType.DMA((len(blocks) + 4,)),
        ],
        compiler_params=PARAMS,
        name="middle",
    )(in_vmem(full), *blocks, *patterns)


def purify(full, rows, square, low, blocks):
    edge, order = square.shape
    return pl.pallas_call(
        purify_kernel,
        out_shape=(
            jax.ShapeDtypeStruct((edge, edge), BF16),
            pltpu.VMEM((order, order), BF16),
            pltpu.VMEM((edge, order), F32),
            pltpu.VMEM((edge, order), BF16),
        ),
        in_specs=[VMEM] * 4 + [HBM] * len(blocks),
        out_specs=(HBM,) + (VMEM,) * 3,
        input_output_aliases={0: 1, 2: 2, 3: 3},
        scratch_shapes=[
            pltpu.VMEM((edge, edge), BF16),
            pltpu.SemaphoreType.DMA((len(blocks),)),
            pltpu.SemaphoreType.DMA((2,)),
        ],
        compiler_params=PARAMS,
        name="purify",
    )(*map(in_vmem, (full, rows, square, low)), *blocks)[0]


def block_body(own, pattern):
    i, j = lax.axis_index("wide"), lax.axis_index("narrow")
    kind = jnp.bitwise_xor(i, j)
    hold = lax.optimization_barrier
    line, across = send(own, LINE), send(own, ACROSS)
    near = send(jnp.where(kind == 0, own, across), NEAR_DIAGONAL)
    far = send(across, FAR_DIAGONAL)
    own_c, across_c = send(own, CORES), send(across, CORES)
    own_c, across_c, line = hold((own_c, across_c, line))
    line_across, last = send(line, ACROSS), send(line, LAST_DIAGONAL)
    line_c = send(line, CORES)
    pattern, line = hold((pattern, line))
    got = {k: lax.ppermute(pattern, "narrow", [(c, c ^ k) for c in range(4)]) for k in (1, 2, 3)}
    patterns = [pattern, got[1], got[2], got[3]]
    full = early((own, own_c, across, across_c, line, line_c))
    patterns, full = hold((patterns, full))
    line_across, full = hold((line_across, full))
    line_across_c = send(line_across, CORES)
    diagonal = jnp.where(kind == 3, last, jnp.where(kind == 1, far, near))
    diagonal_c = send(diagonal, CORES)
    full, rows, square, low = middle(full, (line_across, diagonal, diagonal_c), patterns)
    return purify(full, rows, square, low, (line_across_c,))


def solution(mesh):
    four = mesh.shape["wide"] == 4 and mesh.shape["narrow"] == 4

    def body(density, pattern):
        rows, cols = density.shape
        fits = rows == cols and rows % 128 == 0 and rows <= 512
        fits = fits and pattern.shape[0] == pattern.shape[1] <= 16
        fits = fits and pattern.shape[0] % 2 == 0
        return (block_body if four and fits else panel_body)(density, pattern)

    return jax.shard_map(
        body,
        mesh=mesh,
        in_specs=(P(("groups", "wide"), "narrow"), P(("groups", "wide"), "narrow")),
        out_specs=P(("groups", "wide"), "narrow"),
        check_vma=False,
    )
```
